512 devices in a mesh: req: 8 (over y), head: 8 (over z), exp: 8 (over x, core).
Axes of the slice: x: 4, y: 8, z: 8, core: 2. Of those that a mesh axis runs over, the one named last changes fastest.
Arguments:
- query: bfloat16 [2, 512, 3072], P(None, ('req', 'exp'), 'head'), may hold values from -125 to 125
- cache_keys: bfloat16 [2, 512, 32, 1024], P(None, ('req', 'exp'), None, 'head'), may hold values from -5 to 5
- cache_values: bfloat16 [2, 512, 32, 1024], P(None, ('req', 'exp'), None, 'head'), may hold values from -12 to 12
- lengths: int32 [2, 512], P(None, ('req', 'exp')), may hold values from 2 to 32, as said below
- out_proj: bfloat16 [3072, 3072], P('head', 'exp'), may hold values from -0.109375 to 0.109375
- residual: bfloat16 [2, 512, 3072], P(None, ('req', 'head'), 'exp'), may hold values from -3 to 3
- norm_gain: bfloat16 [3072], P('exp'), may hold values from 0.099609375 to 1.8984375
- router: bfloat16 [3072, 8], P('exp'), may hold values from -0.109375 to 0.109375
- expert_ids: int32 [2, 512, 2], P(None, ('req', 'head')), may hold values from 0 to 7, all different within a row; in each aligned block of 8 rows (0 to 7, 8 to 15, ..., all dimensions but the last counted through in order) at most 4 rows name the same one
- gate_weight: bfloat16 [8, 3072, 16384], P('exp', None, ('req', 'head')), may hold values from -0.109375 to 0.109375
- up_weight: bfloat16 [8, 3072, 16384], P('exp', None, ('req', 'head')), may hold values from -0.109375 to 0.109375
- down_weight: bfloat16 [8, 16384, 3072], P('exp', 'req', 'head'), may hold values from -0.046875 to 0.046875
Outputs:
- layer_out: bfloat16 [2, 512, 3072], P(None, ('req', 'head'), 'exp')
The draws below stay inside these ranges and needn't reach their ends.
Inputs may be any that keep to these rules, and one draw needn't show every extreme that they name: `lengths`: positions at or past a request's length are not read; in every micro-batch some request has all 32 positions valid. `expert_ids`: A token names 2 different experts. Within each aligned block of 8 tokens of a micro-batch (one group), no expert is named more than 4 times, a bound that some block reaches.
All inputs are finite; a program needn't handle non-finite values.
Results may differ from the reference program's by a relative error of at most 0.0068.
Values may be sent and summed in bfloat16 or wider, within the bound.
A program may use at most 64 MiB of HBM per device.

```python
import math
import jax
import jax.numpy as jnp
import numpy as np
from jax import lax

D = 3072
HEADS = 24
KV_HEADS = 8
HEAD_DIM = 128
FF = 16384
TOP = 2
MICRO = 2
TOK_GRP = 8
LMAX = 32
EXPERTS = 8
TOKENS = 512
CAP = 4


def key_slab(key, position):
    drawn = jax.random.normal(jax.random.fold_in(key, position), (MICRO, TOKENS, KV_HEADS * HEAD_DIM), jnp.float32)
    return jnp.clip(drawn, -5.0, 5.0)


def draw_cache_keys(key, part):
    key_slabs = lax.map(lambda position: key_slab(key, position), jnp.arange(LMAX, dtype=jnp.int32))
    return jnp.moveaxis(key_slabs, 0, 2).astype(jnp.bfloat16)


def draw_query(key, part):
    key = jax.random.fold_in(key, 77777)
    drawn = jnp.clip(jax.random.normal(key, (MICRO, TOKENS, HEADS * HEAD_DIM), jnp.float32), -6.0, 6.0)
    return drawn.astype(jnp.bfloat16)


def draw_lengths(key, part):
    key = jax.random.fold_in(key, 90001)
    groups = TOKENS // TOK_GRP
    upper_bound = jax.random.randint(jax.random.fold_in(key, 1), (MICRO, groups, 1), LMAX // 4, LMAX + 1)
    raw_draw = jax.random.randint(jax.random.fold_in(key, 2), (MICRO, groups, TOK_GRP), 0, 1 << 20)
    drawn_lengths = (2 + raw_draw % (upper_bound - 1)).reshape(MICRO, TOKENS)
    longest = jax.random.randint(jax.random.fold_in(key, 3), (MICRO, 1), 0, TOKENS)
    drawn_lengths = jnp.where(jnp.arange(TOKENS, dtype=jnp.int32)[None, :] == longest, LMAX, drawn_lengths)
    return drawn_lengths.astype(jnp.int32)


def shard_levels(key, shape, cuts, least, top_value):
    level = 1.0
    for axis_at, shards_of in cuts:
        draws = jax.random.uniform(jax.random.fold_in(jax.random.fold_in(key, 6), axis_at), (shards_of,), jnp.float32, least / len(cuts), top_value / len(cuts))
        level = level * jnp.repeat(jnp.exp(draws), shape[axis_at] // shards_of).reshape((-1,) + (1,) * (len(shape) - 1 - axis_at))
    return level


def shared_out(key, own, number, rows, count, top, reach, lean):
    order = jax.random.permutation(key, count)
    heavy_load, usual = shares(count, rows * top, reach, lean, True), shares(count, rows * top, reach, lean, False)
    places = jnp.arange(count)

    def named(sizes, rotation):
        used = int((sizes > 0).sum())
        fixed = max(1, used // 4)
        passed = fixed + (places - fixed + rotation * (used - fixed)) % max(1, count - fixed)
        return jnp.zeros((count,), jnp.int32).at[order[jnp.where(places < fixed, places, passed)]].set(jnp.asarray(sizes, jnp.int32))

    sizes = jnp.where(number % 4 == 0, named(heavy_load, number // 4), named(usual, number - number // 4 - 1))
    mixed = jax.random.permutation(jax.random.fold_in(own, 3), count)
    giver, receiver = mixed[0:count // 2 * 2:2], mixed[1:count // 2 * 2:2]
    margin = jnp.minimum(sizes[giver] - 1, reach - sizes[receiver]) // 2
    margin = jnp.where((giver == order[0]) | (receiver == order[0]) | (sizes[receiver] == 0), 0, jnp.maximum(margin, 0))
    passed = jax.random.randint(jax.random.fold_in(own, 4), (count // 2,), 0, 1 << 20) % (margin + 1)
    sizes = sizes.at[giver].add(-passed).at[receiver].add(passed)
    members = jnp.searchsorted(jnp.cumsum(sizes), jnp.arange(rows * top), side="right").astype(jnp.int32)
    listing = members.reshape(top, rows).T
    listing = listing[jax.random.permutation(jax.random.fold_in(own, 1), rows)]
    rotation = jax.random.randint(jax.random.fold_in(own, 2), (rows, 1), 0, top)
    return jnp.take_along_axis(listing, (jnp.arange(top)[None, :] + rotation) % top, axis=1)


def shares(amount, total, bound, slope, full):
    weights = [(1 << 20) // math.isqrt(grade ** slope) + 1 for grade in range(1, amount + 1)]
    largest = bound if full else min(bound, max(-(-total // amount), total * weights[0] // sum(weights)))
    least = 1 if total - largest >= amount - 1 else 0
    holding, spare = [largest] + [least] * (amount - 1), total - largest - least * (amount - 1)
    while spare > 0:
        candidates = [i for i in range(1, amount) if holding[i] < largest] or [i for i in range(1, amount) if holding[i] < bound]
        whole, remaining = sum([weights[i] for i in candidates]), spare
        for i in candidates:
            extra = min(bound - holding[i], max(1, remaining * weights[i] // whole), spare)
            holding[i] = holding[i] + extra
            spare = spare - extra
    return np.array(holding)


def gaussian(key, shape, deviation, bound, shards=(), kind=jnp.bfloat16):
    entries = jax.random.normal(key, shape, jnp.float32) * deviation
    if len(shards) > 0:
        entries = shard_levels(key, shape, shards, -0.22, 0.18) * entries
    return jnp.clip(entries, min=-bound, max=bound).astype(kind)


def setup_inputs(seed: int = 0) -> dict:
    key_of = jax.random.split(jax.random.key(seed), 13)
    query = draw_query(jax.random.fold_in(key_of[12], 71), 0)
    cache_keys = draw_cache_keys(jax.random.fold_in(key_of[12], 71), 0)
    cache_values = gaussian(key_of[2], (MICRO, TOKENS, LMAX, KV_HEADS * HEAD_DIM), 3.0, 12.0, ((1, 64), (3, 8)))
    lengths = draw_lengths(jax.random.fold_in(key_of[12], 71), 0)
    out_proj = gaussian(key_of[4], (HEADS * HEAD_DIM, D), (HEADS * HEAD_DIM) ** -0.5, 0.109375, ((0, 8), (1, 8)))
    residual = gaussian(key_of[5], (MICRO, TOKENS, D), 0.5, 3.0, ((1, 64), (2, 8)))
    norm_gain = jnp.clip(1.0 + 0.18 * jax.random.normal(key_of[6], (D,), jnp.float32), 0.099609375, 1.8984375).astype(jnp.bfloat16)
    router = gaussian(key_of[7], (D, EXPERTS), D ** -0.5, 0.109375, ((0, 8),))
    expert_ids_keys = jax.random.split(jax.random.fold_in(key_of[8], 1), MICRO * TOKENS // TOK_GRP)
    expert_ids_turns = jax.random.permutation(jax.random.fold_in(key_of[8], 3), MICRO * TOKENS // TOK_GRP)
    expert_ids = jax.vmap(lambda own, number: shared_out(jax.random.fold_in(key_of[8], 2), own, number, TOK_GRP, EXPERTS, TOP, CAP, 2))(expert_ids_keys, expert_ids_turns).reshape((MICRO, TOKENS, TOP))
    gate_weight = gaussian(key_of[9], (EXPERTS, D, FF), D ** -0.5, 0.109375, ((0, 8), (2, 64)))
    up_weight = gaussian(key_of[10], (EXPERTS, D, FF), D ** -0.5, 0.109375, ((0, 8), (2, 64)))
    down_weight = gaussian(key_of[11], (EXPERTS, FF, D), FF ** -0.5, 0.046875, ((0, 8), (1, 8), (2, 8)))
    return dict(query=query, cache_keys=cache_keys, cache_values=cache_values, lengths=lengths, out_proj=out_proj, residual=residual, norm_gain=norm_gain, router=router, expert_ids=expert_ids, gate_weight=gate_weight, up_weight=up_weight, down_weight=down_weight)


def attend(query_rows, key_rows, value_rows, lengths_now):
    row_count = query_rows.shape[0]
    positions = key_rows.shape[1]
    key_heads = key_rows.shape[2] // HEAD_DIM
    per_group = query_rows.shape[1] // (key_heads * HEAD_DIM)
    queries = query_rows.astype(jnp.float32).reshape(row_count, key_heads, per_group, HEAD_DIM)
    keys_split = key_rows.astype(jnp.float32).reshape(row_count, positions, key_heads, HEAD_DIM)
    values_split = value_rows.astype(jnp.float32).reshape(row_count, positions, key_heads, HEAD_DIM)
    scores = jnp.einsum('tjgd,tljd->tjgl', queries, keys_split) * HEAD_DIM ** (-0.5)
    allowed = jnp.arange(positions, dtype=jnp.int32)[None, :] < lengths_now[:, None]
    scores = jnp.where(allowed[:, None, None, :], scores, jnp.float32(-1e+30))
    highest = lax.optimization_barrier(jnp.max(scores, axis=-1, keepdims=True))
    exponents = jnp.exp(scores - highest)
    weights_now = (exponents / lax.optimization_barrier(jnp.sum(exponents, axis=-1, keepdims=True))).astype(jnp.bfloat16)
    mixed_out = jnp.einsum('tjgl,tljd->tjgd', weights_now.astype(jnp.float32), values_split)
    return mixed_out.reshape(row_count, key_heads * per_group * HEAD_DIM).astype(jnp.bfloat16)

def route_slots(ids_rows):
    onehot = (ids_rows[:, :, None] == jnp.arange(EXPERTS, dtype=jnp.int32)).astype(jnp.int32)
    member = lax.optimization_barrier(jnp.sum(onehot, axis=1)).reshape(-1, TOK_GRP, EXPERTS)
    earlier = (jnp.cumsum(member, axis=1) - member).reshape(-1, EXPERTS)
    return lax.optimization_barrier(jnp.sum(onehot * earlier[:, None, :], axis=-1)).astype(jnp.int32)

def reference(query, cache_keys, cache_values, lengths, out_proj, residual, norm_gain, router, expert_ids, gate_weight, up_weight, down_weight):
    groups_all = TOKENS // TOK_GRP
    outputs = []
    for micro_index in range(MICRO):
        attended = attend(query[micro_index], cache_keys[micro_index], cache_values[micro_index], lengths[micro_index])
        projected = jnp.dot(attended, out_proj, preferred_element_type=jnp.float32)
        stream = (residual[micro_index].astype(jnp.float32) + projected).astype(jnp.bfloat16)
        stream_full = stream.astype(jnp.float32)
        inverse = lax.rsqrt(lax.optimization_barrier(jnp.sum(stream_full * stream_full, axis=-1)) / D + 1e-05)
        scaled = stream_full * norm_gain.astype(jnp.float32)
        normed_full = scaled * inverse[:, None]
        normed = normed_full.astype(jnp.bfloat16)
        logits = jnp.dot(normed_full, router.astype(jnp.float32), precision=lax.Precision.HIGHEST)
        chosen_ids = expert_ids[micro_index]
        chosen = jnp.take_along_axis(logits, chosen_ids, axis=1)
        exponents = jnp.exp(chosen)
        mixing = exponents / lax.optimization_barrier(jnp.sum(exponents, axis=1, keepdims=True))
        slots = route_slots(chosen_ids)
        owner_rows = (jnp.arange(TOKENS, dtype=jnp.int32) // TOK_GRP).astype(jnp.int32)
        owners = jnp.repeat(owner_rows, TOP)
        buffer = jnp.zeros((EXPERTS, groups_all, CAP, D), jnp.bfloat16)
        buffer = buffer.at[chosen_ids.reshape(-1), owners, slots.reshape(-1)].set(jnp.repeat(normed, TOP, axis=0))

        def expert_out(operands):
            row_block, gate_local, up_local, down_local = operands
            flat_rows = row_block.reshape(groups_all * CAP, D)
            gate_act = jnp.dot(flat_rows, gate_local, preferred_element_type=jnp.float32)
            up_act = jnp.dot(flat_rows, up_local, preferred_element_type=jnp.float32)
            hidden = (jax.nn.silu(gate_act) * up_act).astype(jnp.bfloat16)
            expert_rows = jnp.dot(hidden, down_local, preferred_element_type=jnp.float32).astype(jnp.bfloat16)
            return expert_rows.reshape(groups_all, CAP, D)
        expert_outputs = lax.map(expert_out, (buffer, gate_weight, up_weight, down_weight))
        owner_pairs = jnp.broadcast_to(owner_rows[:, None], (TOKENS, TOP))
        picked = expert_outputs[chosen_ids, owner_pairs, slots].astype(jnp.float32)
        expert_mix = lax.optimization_barrier(jnp.sum(mixing[:, :, None] * picked, axis=1))
        outputs.append((stream_full + expert_mix).astype(jnp.bfloat16))
    return jnp.stack(outputs)
```

```python
import functools

import jax
import jax.numpy as jnp
from jax import lax
from jax.experimental import pallas as pl
from jax.experimental.pallas import tpu as pltpu
from jax.sharding import PartitionSpec as P

MESH = pl.DeviceIdType.MESH
HEAD_DIM = 128
SLOTS = 4
F32 = jnp.float32
BF16 = jnp.bfloat16
EXACT = lax.Precision.HIGHEST


def iota(shape, axis):
    return lax.broadcasted_iota(jnp.int32, shape, axis)


def dot(a, b, **kw):
    return jnp.dot(a, b, preferred_element_type=F32, **kw)


def dot_t(a, b, **kw):
    return lax.dot_general(a, b, (((1,), (1,)), ((), ())), preferred_element_type=F32, **kw)


class Swap:
    def __init__(self, axis, me, n, src, dst, send_sem, recv_sem):
        self.axis, self.me, self.n, self.src, self.dst = axis, me, n, src, dst
        self.send_sem, self.recv_sem = send_sem, recv_sem

    def copy(self, d, to, at):
        return pltpu.make_async_remote_copy(
            src_ref=self.src(to),
            dst_ref=self.dst(at),
            send_sem=self.send_sem.at[d - 1],
            recv_sem=self.recv_sem.at[d - 1],
            device_id={self.axis: to},
            device_id_type=MESH,
        )

    def start(self):
        for d in range(1, self.n):
            self.copy(d, lax.rem(self.me + d, self.n), self.me).start()

    def wait_recv(self):
        for d in range(1, self.n):
            source = lax.rem(self.me + self.n - d, self.n)
            self.copy(d, source, source).wait_recv()

    def wait_send(self):
        for d in range(1, self.n):
            self.copy(d, lax.rem(self.me + d, self.n), self.me).wait_send()


class Ring:
    def __init__(self, axis, me, n, part, sems):
        self.axis, self.me, self.n, self.part, self.sems = axis, me, n, part, sems
        self.half = n // 2

    def parts(self, way, k):
        if k == self.half:
            return (0,) if way == 0 else (1,)
        return (0, 1)

    def block(self, way, k):
        return lax.rem(self.me + (self.n - k if way == 0 else k), self.n)

    def copy(self, way, k, s):
        to = lax.rem(self.me + (1 if way == 0 else self.n - 1), self.n)
        at = 2 * (k - 1) + (s if k < self.half else 0)
        send_sem, recv_sem = self.sems[2 * way], self.sems[2 * way + 1]
        ref = self.part(self.block(way, k - 1), s)
        return pltpu.make_async_remote_copy(
            src_ref=ref,
            dst_ref=ref,
            send_sem=send_sem.at[at],
            recv_sem=recv_sem.at[at],
            device_id={self.axis: to},
            device_id_type=MESH,
        )

    def arrival(self, way, k, s):
        to = lax.rem(self.me + (1 if way == 0 else self.n - 1), self.n)
        at = 2 * (k - 1) + (s if k < self.half else 0)
        send_sem, recv_sem = self.sems[2 * way], self.sems[2 * way + 1]
        ref = self.part(self.block(way, k), s)
        return pltpu.make_async_remote_copy(
            src_ref=ref,
            dst_ref=ref,
            send_sem=send_sem.at[at],
            recv_sem=recv_sem.at[at],
            device_id={self.axis: to},
            device_id_type=MESH,
        )

    def start(self, s):
        for way in (0, 1):
            if s in self.parts(way, 1):
                self.copy(way, 1, s).start()

    def take(self, way, k, s):
        self.arrival(way, k, s).wait_recv()
        if k < self.half and s in self.parts(way, k + 1):
            self.copy(way, k + 1, s).start()

    def step(self, k):
        for s in (0, 1):
            for way in (0, 1):
                if s in self.parts(way, k):
                    self.take(way, k, s)

    def wait_send(self):
        for k in range(1, self.half + 1):
            for way in (0, 1):
                for s in self.parts(way, k):
                    self.copy(way, k, s).wait_send()


def layer(
    n,
    query_ref,
    keys_hbm,
    values_hbm,
    lengths_ref,
    proj_hbm,
    residual_ref,
    aux_ref,
    ids_ref,
    gate_hbm,
    up_hbm,
    down_hbm,
    out_ref,
    keys,
    values,
    proj,
    wide,
    down,
    aux_all,
    att_all,
    part_own,
    part_send,
    part_recv,
    stream_all,
    first_a,
    first_b,
    rows_a,
    rows_b,
    acc_a,
    acc_b,
    hidden,
    acc,
    down_send,
    down_recv,
    back_send,
    back_recv,
    load_sem,
    aux_sem,
    att_sem,
    part_sem,
    stream_sem,
    first_a_sem,
    first_b_sem,
    ring_a_sem,
    ring_b_sem,
    ring_h_sem,
    down_sem,
    back_sem,
):
    micro, group, width = query_ref.shape
    tokens = micro * group
    slots = micro * SLOTS
    r, h, e = lax.axis_index("req"), lax.axis_index("head"), lax.axis_index("exp")
    features = n * width
    hidden_width = gate_hbm.shape[2]
    positions = keys_hbm.shape[2]

    barrier = pltpu.get_barrier_semaphore()
    for axis, me in (("exp", e), ("head", h), ("req", r)):
        for d in range(1, n):
            pl.semaphore_signal(
                barrier, inc=1, device_id={axis: lax.rem(me + d, n)}, device_id_type=MESH
            )
    for j in range(n):

        @pl.when(jnp.logical_or(h != e, e != j))
        def _():
            pl.semaphore_signal(
                barrier, inc=1, device_id={"head": e, "exp": jnp.int32(j)}, device_id_type=MESH
            )

    loads = [
        pltpu.make_async_copy(keys_hbm, keys, load_sem.at[0]),
        pltpu.make_async_copy(values_hbm, values, load_sem.at[1]),
        pltpu.make_async_copy(proj_hbm, proj, load_sem.at[2]),
        pltpu.make_async_copy(gate_hbm.at[0], wide.at[:, pl.ds(0, hidden_width)], load_sem.at[3]),
        pltpu.make_async_copy(
            up_hbm.at[0], wide.at[:, pl.ds(hidden_width, hidden_width)], load_sem.at[4]
        ),
        pltpu.make_async_copy(down_hbm.at[0], down, load_sem.at[5]),
    ]
    for load in loads:
        load.start()

    per_key = width // HEAD_DIM
    queries = query_ref[...].astype(F32).reshape(tokens, width)
    queries = jnp.concatenate(
        [queries[:, j * HEAD_DIM : (j + 1) * HEAD_DIM] for j in range(per_key)], axis=0
    ).astype(BF16)
    columns = tokens * positions
    owner = iota((1, columns), 1) // positions
    limit = jnp.zeros((1, columns), jnp.int32)
    for t in range(tokens):
        limit = jnp.where(owner == t, lengths_ref[t // group, t % group], limit)
    valid = lax.rem(iota((1, columns), 1), positions) < limit
    owner = jnp.where(valid, owner, -1)
    allowed = lax.rem(iota((per_key * tokens, columns), 0), tokens) == owner
    loads[0].wait()
    scores = dot_t(queries, keys[...].reshape(columns, HEAD_DIM)) * HEAD_DIM ** (-0.5)
    scores = jnp.where(allowed, scores, F32(-1e30))
    exponents = jnp.exp(scores - jnp.max(scores, axis=-1, keepdims=True))
    weights = (exponents / jnp.sum(exponents, axis=-1, keepdims=True)).astype(BF16)
    loads[1].wait()
    mixed = dot(weights, values[...].reshape(columns, HEAD_DIM))
    for j in range(per_key):
        att_all[e, :, j * HEAD_DIM : (j + 1) * HEAD_DIM] = mixed[
            j * tokens : (j + 1) * tokens
        ].astype(BF16)
    aux_all[e] = aux_ref[...]

    pl.semaphore_wait(barrier, 3 * (n - 1) + n - jnp.where(h == e, 1, 0))

    swap_att = Swap("exp", e, n, lambda to: att_all.at[e], lambda at: att_all.at[at], *att_sem)
    swap_aux = Swap("exp", e, n, lambda to: aux_all.at[e], lambda at: aux_all.at[at], *aux_sem)
    swap_att.start()
    swap_aux.start()

    places = n * slots
    ids = [
        jnp.concatenate([ids_ref[m][:, k : k + 1] for m in range(micro)], axis=0) for k in range(2)
    ]
    token_at = iota((tokens, places), 0)
    column = iota((tokens, places), 1)
    hots = [(ids[k] == column // slots).astype(F32) for k in range(2)]
    earlier_of = (
        (iota((tokens, tokens), 1) < iota((tokens, tokens), 0))
        & (iota((tokens, tokens), 1) // group == iota((tokens, tokens), 0) // group)
    ).astype(BF16)
    earlier = dot(earlier_of, (hots[0] + hots[1]).astype(BF16))
    fits = (lax.rem(column, SLOTS).astype(F32) == earlier) & (
        lax.rem(column, slots) // SLOTS == token_at // group
    )
    chosen_at = [jnp.where(fits, hot, F32(0.0)) for hot in hots]
    sel_own = dot_t(
        ((iota((slots, places), 1) - slots * e) == iota((slots, places), 0)).astype(BF16),
        (chosen_at[0] + chosen_at[1]).astype(BF16),
    ).astype(BF16)

    loads[2].wait()
    swap_att.wait_recv()
    partial = dot(att_all[...].reshape(n * tokens, width), proj[...]).reshape(n, tokens, width)
    part_own[...] = partial
    part_send[...] = partial.astype(BF16)
    swap_part = Swap(
        "head", h, n, lambda to: part_send.at[to], lambda at: part_recv.at[at], *part_sem
    )
    swap_part.start()
    projected = part_own[h]
    residual = residual_ref[...].astype(F32).reshape(tokens, width)
    swap_part.wait_recv()
    for d in range(1, n):
        projected += part_recv[lax.rem(h + d, n)].astype(F32)
    stream_all[e] = (residual + projected).astype(BF16)
    swap_stream = Swap(
        "exp", e, n, lambda to: stream_all.at[e], lambda at: stream_all.at[at], *stream_sem
    )
    swap_stream.start()
    swap_aux.wait_recv()
    swap_stream.wait_recv()

    squares = jnp.zeros((tokens, width), F32)
    for j in range(n):
        block = stream_all[j].astype(F32)
        squares += block * block
    inverse = lax.rsqrt(jnp.sum(squares, axis=-1, keepdims=True) / features + 1e-05)
    normed = []
    for j in range(n):
        full = stream_all[j].astype(F32) * aux_all[j].astype(F32)[n : n + 1] * inverse
        normed.append(full)
    quarter = n // 4
    rows = [dot(sel_own, normed[j].astype(BF16)) for j in range(n)]
    for i in range(quarter):
        at = pl.ds(i * width, width)
        first_a[h, :, at] = jnp.concatenate([rows[i], rows[quarter + i]], axis=0).astype(BF16)
        first_b[r, :, at] = jnp.concatenate(
            [rows[2 * quarter + i], rows[3 * quarter + i]], axis=0
        ).astype(BF16)
    swap_a = Swap("head", h, n, lambda to: first_a.at[h], lambda at: first_a.at[at], *first_a_sem)
    swap_b = Swap("req", r, n, lambda to: first_b.at[r], lambda at: first_b.at[at], *first_b_sem)
    swap_a.start()
    swap_b.start()

    logits = jnp.zeros((tokens, 2 * n), F32)
    for j in range(n):
        logits += dot_t(normed[j], aux_all[j].astype(F32), precision=EXACT)
    lane = iota((tokens, 2 * n), 1)
    powers = [
        jnp.exp(jnp.sum(jnp.where(lane == ids[k], logits, F32(0.0)), axis=-1, keepdims=True))
        for k in range(2)
    ]
    total = powers[0] + powers[1]
    mixing = powers[0] / total * chosen_at[0] + powers[1] / total * chosen_at[1]

    half = features // 2
    quarter_width = half // 2

    def settle(first, rows_to, at):
        for i in range(n // 2):
            x, y = first[2 * i].astype(F32), first[2 * i + 1].astype(F32)
            for c in range(2):
                rows_to[
                    at, pl.ds(2 * slots * i, 2 * slots), pl.ds(c * quarter_width, quarter_width)
                ] = jnp.concatenate(
                    [x[c * slots : (c + 1) * slots], y[c * slots : (c + 1) * slots]], axis=0
                ).astype(BF16)

    block_rows = n * slots
    part_rows = block_rows // 2
    ring_a = Ring(
        "req", r, n, lambda b, s: rows_a.at[b, pl.ds(s * part_rows, part_rows)], ring_a_sem
    )
    ring_b = Ring(
        "head", h, n, lambda b, s: rows_b.at[b, pl.ds(s * part_rows, part_rows)], ring_b_sem
    )
    swap_a.wait_recv()
    settle(first_a, rows_a, r)
    ring_a.start(0)
    ring_a.start(1)
    swap_b.wait_recv()
    settle(first_b, rows_b, h)
    ring_b.start(0)
    ring_b.start(1)
    loads[3].wait()
    loads[4].wait()

    def product(rows_from, top, blocks):
        x = [rows_from[b] for b in blocks]
        x = x[0] if len(x) == 1 else jnp.concatenate(x, axis=0)
        return dot(x, wide[pl.ds(top, half), :])

    def multiply(blocks_a, blocks_b):
        y = product(rows_a, 0, blocks_a)
        for i, b in enumerate(blocks_a):
            acc_a[b] = y[i * block_rows : (i + 1) * block_rows]
        y = product(rows_b, half, blocks_b)
        for i, b in enumerate(blocks_b):
            acc_b[b] = y[i * block_rows : (i + 1) * block_rows].reshape(n, slots, 2 * hidden_width)

    multiply([r], [h])
    for k in range(1, n // 2 + 1):
        ring_a.step(k)
        ring_b.step(k)
        ways = (0, 1) if k < n // 2 else (0,)
        multiply([ring_a.block(w, k) for w in ways], [ring_b.block(w, k) for w in ways])

    ring_h = Ring("head", h, n, lambda b, s: hidden.at[b, pl.ds(s * (n // 2), n // 2)], ring_h_sem)

    def activate(b):
        both = acc_a[b] + acc_b[:, b].reshape(block_rows, 2 * hidden_width)
        gated, upward = both[:, :hidden_width], both[:, hidden_width:]
        hidden[h, b] = (gated / (1.0 + jnp.exp(-gated)) * upward).astype(BF16)

    for s in range(2):
        for b in range(s * (n // 2), (s + 1) * (n // 2)):
            activate(b)
        ring_h.start(s)
    loads[5].wait()

    def lower(b, s, first=False):
        at = pl.ds(s * (n // 2), n // 2)
        x = hidden[b, at].reshape(n // 2 * block_rows, hidden_width)
        y = dot(x, down[pl.ds(pl.multiple_of(b * hidden_width, hidden_width), hidden_width), :])
        y = y.reshape(n // 2, block_rows, width)
        acc[at] = y if first else acc[at] + y

    lower(h, 0, True)
    lower(h, 1, True)
    for k in range(1, n // 2 + 1):
        ring_h.step(k)
        for s in range(2):
            for way in (0, 1):
                if s in ring_h.parts(way, k):
                    lower(ring_h.block(way, k), s)

    down_send[...] = acc[...].astype(BF16)
    swap_down = Swap(
        "req", r, n, lambda to: down_send.at[to], lambda at: down_recv.at[at], *down_sem
    )
    swap_down.start()
    expert_rows = acc[r]
    swap_down.wait_recv()
    for d in range(1, n):
        expert_rows += down_recv[lax.rem(r + d, n)].astype(F32)
    back_send[...] = expert_rows.reshape(n, slots, width)

    def back(to, at):
        return pltpu.make_async_remote_copy(
            src_ref=back_send.at[to],
            dst_ref=back_recv.at[at],
            send_sem=back_sem[0].at[to],
            recv_sem=back_sem[1].at[at],
            device_id={"head": jnp.int32(to), "exp": h},
            device_id_type=MESH,
        )

    for j in range(n):

        @pl.when(jnp.logical_or(h != e, h != j))
        def _():
            back(j, e).start()

        @pl.when(jnp.logical_and(h == e, h == j))
        def _():
            back_recv[j] = back_send[j]

    for j in range(n):

        @pl.when(jnp.logical_or(h != e, e != j))
        def _():
            back(j, j).wait_recv()

    returned = back_recv[...].reshape(places, width).astype(BF16).astype(F32)
    result = stream_all[e].astype(F32) + dot(mixing, returned, precision=EXACT)
    out_ref[...] = result.reshape(micro, group, width).astype(BF16)

    for swap in (swap_att, swap_aux, swap_part, swap_stream, swap_a, swap_b, swap_down):
        swap.wait_send()
    for ring in (ring_a, ring_b, ring_h):
        ring.wait_send()
    for j in range(n):

        @pl.when(jnp.logical_or(h != e, h != j))
        def _():
            back(j, e).wait_send()


def per_device(
    n,
    query,
    cache_keys,
    cache_values,
    lengths,
    out_proj,
    residual,
    norm_gain,
    router,
    expert_ids,
    gate_weight,
    up_weight,
    down_weight,
):
    micro, group, width = query.shape
    tokens, slots = micro * group, micro * SLOTS
    features = n * width
    hidden_width = gate_weight.shape[2]
    aux = jnp.concatenate(
        [router.T, norm_gain[None, :], jnp.zeros((n - 1, width), BF16)], axis=0
    )
    vmem = pl.BlockSpec(memory_space=pltpu.VMEM)
    smem = pl.BlockSpec(memory_space=pltpu.SMEM)
    anywhere = pl.BlockSpec(memory_space=pl.ANY)

    def pair(count):
        return (pltpu.SemaphoreType.DMA((count,)), pltpu.SemaphoreType.DMA((count,)))

    ring = (pltpu.SemaphoreType.DMA((n - 1,)),) * 4
    block_rows = n * slots
    scratch = [
        pltpu.VMEM(cache_keys.shape, BF16),
        pltpu.VMEM(cache_values.shape, BF16),
        pltpu.VMEM(out_proj.shape, BF16),
        pltpu.VMEM((features, 2 * hidden_width), BF16),
        pltpu.VMEM(down_weight.shape[1:], BF16),
        pltpu.VMEM((n, 2 * n, width), BF16),
        pltpu.VMEM((n, tokens, width), BF16),
        pltpu.VMEM((n, tokens, width), F32),
        pltpu.VMEM((n, tokens, width), BF16),
        pltpu.VMEM((n, tokens, width), BF16),
        pltpu.VMEM((n, tokens, width), BF16),
        pltpu.VMEM((n, 2 * slots, features // 4), BF16),
        pltpu.VMEM((n, 2 * slots, features // 4), BF16),
        pltpu.VMEM((n, block_rows, features // 2), BF16),
        pltpu.VMEM((n, block_rows, features // 2), BF16),
        pltpu.VMEM((n, block_rows, 2 * hidden_width), F32),
        pltpu.VMEM((n, n, slots, 2 * hidden_width), F32),
        pltpu.VMEM((n, n, block_rows, hidden_width), BF16),
        pltpu.VMEM((n, block_rows, width), F32),
        pltpu.VMEM((n, block_rows, width), BF16),
        pltpu.VMEM((n, block_rows, width), BF16),
        pltpu.VMEM((n, slots, width), F32),
        pltpu.VMEM((n, slots, width), F32),
        pltpu.SemaphoreType.DMA((6,)),
        pair(n - 1),
        pair(n - 1),
        pair(n - 1),
        pair(n - 1),
        pair(n - 1),
        pair(n - 1),
        ring,
        ring,
        ring,
        pair(n - 1),
        pair(n),
    ]
    return pl.pallas_call(
        functools.partial(layer, n),
        out_shape=jax.ShapeDtypeStruct((micro, group, width), BF16),
        in_specs=[
            vmem,
            anywhere,
            anywhere,
            smem,
            anywhere,
            vmem,
            vmem,
            vmem,
            anywhere,
            anywhere,
            anywhere,
        ],
        out_specs=vmem,
        scratch_shapes=scratch,
        compiler_params=pltpu.CompilerParams(
            collective_id=0, has_side_effects=True, vmem_limit_bytes=48 * 1024 * 1024
        ),
    )(
        query,
        cache_keys,
        cache_values,
        lengths,
        out_proj,
        residual,
        aux,
        expert_ids,
        gate_weight,
        up_weight,
        down_weight,
    )


def solution(mesh):
    in_specs = (
        P(None, ("req", "exp"), "head"),
        P(None, ("req", "exp"), None, "head"),
        P(None, ("req", "exp"), None, "head"),
        P(None, ("req", "exp")),
        P("head", "exp"),
        P(None, ("req", "head"), "exp"),
        P("exp"),
        P("exp", None),
        P(None, ("req", "head"), None),
        P("exp", None, ("req", "head")),
        P("exp", None, ("req", "head")),
        P("exp", "req", "head"),
    )
    out_specs = P(None, ("req", "head"), "exp")
    return jax.shard_map(
        functools.partial(per_device, mesh.shape["exp"]),
        mesh=mesh,
        in_specs=in_specs,
        out_specs=out_specs,
        check_vma=False,
    )
```

```python
import functools

import jax
import jax.numpy as jnp
from jax import lax
from jax.experimental import pallas as pl
from jax.experimental.pallas import tpu as pltpu
from jax.sharding import PartitionSpec as P

MESH = pl.DeviceIdType.MESH
HEAD_DIM = 128
SLOTS = 4
F32 = jnp.float32
BF16 = jnp.bfloat16
EXACT = lax.Precision.HIGHEST


def iota(shape, axis):
    return lax.broadcasted_iota(jnp.int32, shape, axis)


def dot(a, b, **kw):
    return jnp.dot(a, b, preferred_element_type=F32, **kw)


def dot_t(a, b, **kw):
    return lax.dot_general(a, b, (((1,), (1,)), ((), ())), preferred_element_type=F32, **kw)


class Swap:
    def __init__(self, axis, me, n, src, dst, send_sem, recv_sem):
        self.axis, self.me, self.n, self.src, self.dst = axis, me, n, src, dst
        self.send_sem, self.recv_sem = send_sem, recv_sem

    def copy(self, d, to, at):
        return pltpu.make_async_remote_copy(
            src_ref=self.src(to),
            dst_ref=self.dst(at),
            send_sem=self.send_sem.at[d - 1],
            recv_sem=self.recv_sem.at[d - 1],
            device_id={self.axis: to},
            device_id_type=MESH,
        )

    def start(self):
        for d in range(1, self.n):
            self.copy(d, lax.rem(self.me + d, self.n), self.me).start()

    def wait_recv(self):
        for d in range(1, self.n):
            source = lax.rem(self.me + self.n - d, self.n)
            self.copy(d, source, source).wait_recv()

    def wait_send(self):
        for d in range(1, self.n):
            self.copy(d, lax.rem(self.me + d, self.n), self.me).wait_send()


class Ring:
    def __init__(self, axis, me, n, part, sems):
        self.axis, self.me, self.n, self.part, self.sems = axis, me, n, part, sems
        self.half = n // 2

    def parts(self, way, k):
        if k == self.half:
            return (0,) if way == 0 else (1,)
        return (0, 1)

    def block(self, way, k):
        return lax.rem(self.me + (self.n - k if way == 0 else k), self.n)

    def copy(self, way, k, s):
        to = lax.rem(self.me + (1 if way == 0 else self.n - 1), self.n)
        at = 2 * (k - 1) + (s if k < self.half else 0)
        send_sem, recv_sem = self.sems[2 * way], self.sems[2 * way + 1]
        ref = self.part(self.block(way, k - 1), s)
        return pltpu.make_async_remote_copy(
            src_ref=ref,
            dst_ref=ref,
            send_sem=send_sem.at[at],
            recv_sem=recv_sem.at[at],
            device_id={self.axis: to},
            device_id_type=MESH,
        )

    def arrival(self, way, k, s):
        to = lax.rem(self.me + (1 if way == 0 else self.n - 1), self.n)
        at = 2 * (k - 1) + (s if k < self.half else 0)
        send_sem, recv_sem = self.sems[2 * way], self.sems[2 * way + 1]
        ref = self.part(self.block(way, k), s)
        return pltpu.make_async_remote_copy(
            src_ref=ref,
            dst_ref=ref,
            send_sem=send_sem.at[at],
            recv_sem=recv_sem.at[at],
            device_id={self.axis: to},
            device_id_type=MESH,
        )

    def start(self, s):
        for way in (0, 1):
            if s in self.parts(way, 1):
                self.copy(way, 1, s).start()

    def take(self, way, k, s):
        self.arrival(way, k, s).wait_recv()
        if k < self.half and s in self.parts(way, k + 1):
            self.copy(way, k + 1, s).start()

    def step(self, k):
        for s in (0, 1):
            for way in (0, 1):
                if s in self.parts(way, k):
                    self.take(way, k, s)

    def wait_send(self):
        for k in range(1, self.half + 1):
            for way in (0, 1):
                for s in self.parts(way, k):
                    self.copy(way, k, s).wait_send()


def layer(
    n,
    query_ref,
    keys_hbm,
    values_hbm,
    lengths_ref,
    proj_hbm,
    residual_ref,
    gain_ref,
    router_ref,
    ids_ref,
    gate_hbm,
    up_hbm,
    down_hbm,
    out_ref,
    keys,
    values,
    proj,
    wide,
    down,
    aux_all,
    att_all,
    part_own,
    part_send,
    part_recv,
    stream_all,
    first_a,
    first_b,
    rows_a,
    rows_b,
    acc_a,
    acc_b,
    hidden,
    acc,
    down_send,
    down_recv,
    back_send,
    back_recv,
    load_sem,
    aux_sem,
    att_sem,
    part_sem,
    stream_sem,
    first_a_sem,
    first_b_sem,
    ring_a_sem,
    ring_b_sem,
    ring_h_sem,
    down_sem,
    back_sem,
):
    micro, group, width = query_ref.shape
    tokens = micro * group
    slots = micro * SLOTS
    r, h, e = lax.axis_index("req"), lax.axis_index("head"), lax.axis_index("exp")
    features = n * width
    hidden_width = gate_hbm.shape[2]
    positions = keys_hbm.shape[2]

    barrier = pltpu.get_barrier_semaphore()
    for axis, me in (("exp", e), ("head", h), ("req", r)):
        for d in range(1, n):
            pl.semaphore_signal(
                barrier, inc=1, device_id={axis: lax.rem(me + d, n)}, device_id_type=MESH
            )
    for j in range(n):

        @pl.when(jnp.logical_or(h != e, e != j))
        def _():
            pl.semaphore_signal(
                barrier, inc=1, device_id={"head": e, "exp": jnp.int32(j)}, device_id_type=MESH
            )

    loads = [
        pltpu.make_async_copy(keys_hbm, keys, load_sem.at[0]),
        pltpu.make_async_copy(values_hbm, values, load_sem.at[1]),
        pltpu.make_async_copy(proj_hbm, proj, load_sem.at[2]),
        pltpu.make_async_copy(gate_hbm.at[0], wide.at[:, pl.ds(0, hidden_width)], load_sem.at[3]),
        pltpu.make_async_copy(
            up_hbm.at[0], wide.at[:, pl.ds(hidden_width, hidden_width)], load_sem.at[4]
        ),
        pltpu.make_async_copy(down_hbm.at[0], down, load_sem.at[5]),
    ]
    for load in loads:
        load.start()

    per_key = width // HEAD_DIM
    queries = query_ref[...].astype(F32).reshape(tokens, width)
    queries = jnp.concatenate(
        [queries[:, j * HEAD_DIM : (j + 1) * HEAD_DIM] for j in range(per_key)], axis=0
    ).astype(BF16)
    columns = tokens * positions
    owner = iota((1, columns), 1) // positions
    limit = jnp.zeros((1, columns), jnp.int32)
    for t in range(tokens):
        limit = jnp.where(owner == t, lengths_ref[t // group, t % group], limit)
    valid = lax.rem(iota((1, columns), 1), positions) < limit
    owner = jnp.where(valid, owner, -1)
    allowed = lax.rem(iota((per_key * tokens, columns), 0), tokens) == owner
    loads[0].wait()
    scores = dot_t(queries, keys[...].reshape(columns, HEAD_DIM)) * HEAD_DIM ** (-0.5)
    scores = jnp.where(allowed, scores, F32(-1e30))
    exponents = jnp.exp(scores - jnp.max(scores, axis=-1, keepdims=True))
    weights = (exponents / jnp.sum(exponents, axis=-1, keepdims=True)).astype(BF16)
    loads[1].wait()
    mixed = dot(weights, values[...].reshape(columns, HEAD_DIM))
    for j in range(per_key):
        att_all[e, :, j * HEAD_DIM : (j + 1) * HEAD_DIM] = mixed[
            j * tokens : (j + 1) * tokens
        ].astype(BF16)
    gain = jnp.broadcast_to(gain_ref[...].astype(F32).reshape(1, width), (n, width))
    aux_all[e] = jnp.concatenate([router_ref[...].astype(F32), gain], axis=0).astype(BF16)

    pl.semaphore_wait(barrier, 3 * (n - 1) + n - jnp.where(h == e, 1, 0))

    swap_att = Swap("exp", e, n, lambda to: att_all.at[e], lambda at: att_all.at[at], *att_sem)
    swap_aux = Swap("exp", e, n, lambda to: aux_all.at[e], lambda at: aux_all.at[at], *aux_sem)
    swap_att.start()
    swap_aux.start()

    places = n * slots
    diagonal = iota((group, group), 0) == iota((group, group), 1)

    def upright(row):
        return jnp.sum(jnp.where(diagonal, row, F32(0.0)), axis=-1, keepdims=True)

    ids = [
        jnp.concatenate(
            [upright(ids_ref[m][k : k + 1, :].astype(F32)) for m in range(micro)], axis=0
        ).astype(jnp.int32)
        for k in range(2)
    ]
    token_at = iota((tokens, places), 0)
    column = iota((tokens, places), 1)
    hots = [(ids[k] == column // slots).astype(F32) for k in range(2)]
    earlier_of = (
        (iota((tokens, tokens), 1) < iota((tokens, tokens), 0))
        & (iota((tokens, tokens), 1) // group == iota((tokens, tokens), 0) // group)
    ).astype(BF16)
    earlier = dot(earlier_of, (hots[0] + hots[1]).astype(BF16))
    fits = (lax.rem(column, SLOTS).astype(F32) == earlier) & (
        lax.rem(column, slots) // SLOTS == token_at // group
    )
    chosen_at = [jnp.where(fits, hot, F32(0.0)) for hot in hots]
    sel_own = dot_t(
        ((iota((slots, places), 1) - slots * e) == iota((slots, places), 0)).astype(BF16),
        (chosen_at[0] + chosen_at[1]).astype(BF16),
    ).astype(BF16)

    loads[2].wait()
    swap_att.wait_recv()
    partial = dot(att_all[...].reshape(n * tokens, width), proj[...]).reshape(n, tokens, width)
    part_own[...] = partial
    part_send[...] = partial.astype(BF16)
    swap_part = Swap(
        "head", h, n, lambda to: part_send.at[to], lambda at: part_recv.at[at], *part_sem
    )
    swap_part.start()
    projected = part_own[h]
    residual = residual_ref[...].astype(F32).reshape(tokens, width)
    swap_part.wait_recv()
    for d in range(1, n):
        projected += part_recv[lax.rem(h + d, n)].astype(F32)
    stream_all[e] = (residual + projected).astype(BF16)
    swap_stream = Swap(
        "exp", e, n, lambda to: stream_all.at[e], lambda at: stream_all.at[at], *stream_sem
    )
    swap_stream.start()
    swap_aux.wait_recv()
    swap_stream.wait_recv()

    squares = jnp.zeros((tokens, width), F32)
    for j in range(n):
        block = stream_all[j].astype(F32)
        squares += block * block
    inverse = lax.rsqrt(jnp.sum(squares, axis=-1, keepdims=True) / features + 1e-05)
    normed = []
    for j in range(n):
        full = stream_all[j].astype(F32) * aux_all[j].astype(F32)[n : n + 1] * inverse
        normed.append(full)
    quarter = n // 4
    rows = [dot(sel_own, normed[j].astype(BF16)) for j in range(n)]
    for i in range(quarter):
        at = pl.ds(i * width, width)
        first_a[h, :, at] = jnp.concatenate([rows[i], rows[quarter + i]], axis=0).astype(BF16)
        first_b[r, :, at] = jnp.concatenate(
            [rows[2 * quarter + i], rows[3 * quarter + i]], axis=0
        ).astype(BF16)
    swap_a = Swap("head", h, n, lambda to: first_a.at[h], lambda at: first_a.at[at], *first_a_sem)
    swap_b = Swap("req", r, n, lambda to: first_b.at[r], lambda at: first_b.at[at], *first_b_sem)
    swap_a.start()
    swap_b.start()

    logits = jnp.zeros((tokens, 2 * n), F32)
    for j in range(n):
        logits += dot_t(normed[j], aux_all[j].astype(F32), precision=EXACT)
    lane = iota((tokens, 2 * n), 1)
    powers = [
        jnp.exp(jnp.sum(jnp.where(lane == ids[k], logits, F32(0.0)), axis=-1, keepdims=True))
        for k in range(2)
    ]
    total = powers[0] + powers[1]
    mixing = powers[0] / total * chosen_at[0] + powers[1] / total * chosen_at[1]

    half = features // 2
    quarter_width = half // 2

    def settle(first, rows_to, at):
        for i in range(n // 2):
            x, y = first[2 * i].astype(F32), first[2 * i + 1].astype(F32)
            for c in range(2):
                rows_to[
                    at, pl.ds(2 * slots * i, 2 * slots), pl.ds(c * quarter_width, quarter_width)
                ] = jnp.concatenate(
                    [x[c * slots : (c + 1) * slots], y[c * slots : (c + 1) * slots]], axis=0
                ).astype(BF16)

    block_rows = n * slots
    part_rows = block_rows // 2
    ring_a = Ring(
        "req", r, n, lambda b, s: rows_a.at[b, pl.ds(s * part_rows, part_rows)], ring_a_sem
    )
    ring_b = Ring(
        "head", h, n, lambda b, s: rows_b.at[b, pl.ds(s * part_rows, part_rows)], ring_b_sem
    )
    swap_a.wait_recv()
    settle(first_a, rows_a, r)
    ring_a.start(0)
    ring_a.start(1)
    swap_b.wait_recv()
    settle(first_b, rows_b, h)
    ring_b.start(0)
    ring_b.start(1)
    loads[3].wait()
    loads[4].wait()

    def product(rows_from, top, blocks):
        x = [rows_from[b] for b in blocks]
        x = x[0] if len(x) == 1 else jnp.concatenate(x, axis=0)
        return dot(x, wide[pl.ds(top, half), :])

    def multiply(blocks_a, blocks_b):
        y = product(rows_a, 0, blocks_a)
        for i, b in enumerate(blocks_a):
            acc_a[b] = y[i * block_rows : (i + 1) * block_rows]
        y = product(rows_b, half, blocks_b)
        for i, b in enumerate(blocks_b):
            acc_b[b] = y[i * block_rows : (i + 1) * block_rows].reshape(n, slots, 2 * hidden_width)

    multiply([r], [h])
    for k in range(1, n // 2 + 1):
        ring_a.step(k)
        ring_b.step(k)
        ways = (0, 1) if k < n // 2 else (0,)
        multiply([ring_a.block(w, k) for w in ways], [ring_b.block(w, k) for w in ways])

    ring_h = Ring("head", h, n, lambda b, s: hidden.at[b, pl.ds(s * (n // 2), n // 2)], ring_h_sem)

    def activate(b):
        both = acc_a[b] + acc_b[:, b].reshape(block_rows, 2 * hidden_width)
        gated, upward = both[:, :hidden_width], both[:, hidden_width:]
        hidden[h, b] = (gated / (1.0 + jnp.exp(-gated)) * upward).astype(BF16)

    for s in range(2):
        for b in range(s * (n // 2), (s + 1) * (n // 2)):
            activate(b)
        ring_h.start(s)
    loads[5].wait()

    def lower(b, s, first=False):
        at = pl.ds(s * (n // 2), n // 2)
        x = hidden[b, at].reshape(n // 2 * block_rows, hidden_width)
        y = dot(x, down[pl.ds(pl.multiple_of(b * hidden_width, hidden_width), hidden_width), :])
        y = y.reshape(n // 2, block_rows, width)
        acc[at] = y if first else acc[at] + y

    lower(h, 0, True)
    lower(h, 1, True)
    for k in range(1, n // 2 + 1):
        ring_h.step(k)
        for s in range(2):
            for way in (0, 1):
                if s in ring_h.parts(way, k):
                    lower(ring_h.block(way, k), s)

    down_send[...] = acc[...].astype(BF16)
    swap_down = Swap(
        "req", r, n, lambda to: down_send.at[to], lambda at: down_recv.at[at], *down_sem
    )
    swap_down.start()
    expert_rows = acc[r]
    swap_down.wait_recv()
    for d in range(1, n):
        expert_rows += down_recv[lax.rem(r + d, n)].astype(F32)
    back_send[...] = expert_rows.reshape(n, slots, width)

    def back(to, at):
        return pltpu.make_async_remote_copy(
            src_ref=back_send.at[to],
            dst_ref=back_recv.at[at],
            send_sem=back_sem[0].at[to],
            recv_sem=back_sem[1].at[at],
            device_id={"head": jnp.int32(to), "exp": h},
            device_id_type=MESH,
        )

    for j in range(n):

        @pl.when(jnp.logical_or(h != e, h != j))
        def _():
            back(j, e).start()

        @pl.when(jnp.logical_and(h == e, h == j))
        def _():
            back_recv[j] = back_send[j]

    for j in range(n):

        @pl.when(jnp.logical_or(h != e, e != j))
        def _():
            back(j, j).wait_recv()

    returned = back_recv[...].reshape(places, width).astype(BF16).astype(F32)
    result = stream_all[e].astype(F32) + dot(mixing, returned, precision=EXACT)
    out_ref[...] = result.reshape(micro, group, width).astype(BF16)

    for swap in (swap_att, swap_aux, swap_part, swap_stream, swap_a, swap_b, swap_down):
        swap.wait_send()
    for ring in (ring_a, ring_b, ring_h):
        ring.wait_send()
    for j in range(n):

        @pl.when(jnp.logical_or(h != e, h != j))
        def _():
            back(j, e).wait_send()


def per_device(
    n,
    query,
    cache_keys,
    cache_values,
    lengths,
    out_proj,
    residual,
    norm_gain,
    router,
    expert_ids,
    gate_weight,
    up_weight,
    down_weight,
):
    micro, group, width = query.shape
    tokens, slots = micro * group, micro * SLOTS
    features = n * width
    hidden_width = gate_weight.shape[2]
    vmem = pl.BlockSpec(memory_space=pltpu.VMEM)
    smem = pl.BlockSpec(memory_space=pltpu.SMEM)
    anywhere = pl.BlockSpec(memory_space=pl.ANY)

    def pair(count):
        return (pltpu.SemaphoreType.DMA((count,)), pltpu.SemaphoreType.DMA((count,)))

    ring = (pltpu.SemaphoreType.DMA((n - 1,)),) * 4
    block_rows = n * slots
    scratch = [
        pltpu.VMEM(cache_keys.shape, BF16),
        pltpu.VMEM(cache_values.shape, BF16),
        pltpu.VMEM(out_proj.shape, BF16),
        pltpu.VMEM((features, 2 * hidden_width), BF16),
        pltpu.VMEM(down_weight.shape[1:], BF16),
        pltpu.VMEM((n, 2 * n, width), BF16),
        pltpu.VMEM((n, tokens, width), BF16),
        pltpu.VMEM((n, tokens, width), F32),
        pltpu.VMEM((n, tokens, width), BF16),
        pltpu.VMEM((n, tokens, width), BF16),
        pltpu.VMEM((n, tokens, width), BF16),
        pltpu.VMEM((n, 2 * slots, features // 4), BF16),
        pltpu.VMEM((n, 2 * slots, features // 4), BF16),
        pltpu.VMEM((n, block_rows, features // 2), BF16),
        pltpu.VMEM((n, block_rows, features // 2), BF16),
        pltpu.VMEM((n, block_rows, 2 * hidden_width), F32),
        pltpu.VMEM((n, n, slots, 2 * hidden_width), F32),
        pltpu.VMEM((n, n, block_rows, hidden_width), BF16),
        pltpu.VMEM((n, block_rows, width), F32),
        pltpu.VMEM((n, block_rows, width), BF16),
        pltpu.VMEM((n, block_rows, width), BF16),
        pltpu.VMEM((n, slots, width), F32),
        pltpu.VMEM((n, slots, width), F32),
        pltpu.SemaphoreType.DMA((6,)),
        pair(n - 1),
        pair(n - 1),
        pair(n - 1),
        pair(n - 1),
        pair(n - 1),
        pair(n - 1),
        ring,
        ring,
        ring,
        pair(n - 1),
        pair(n),
    ]
    return pl.pallas_call(
        functools.partial(layer, n),
        out_shape=jax.ShapeDtypeStruct((micro, group, width), BF16),
        in_specs=[
            vmem,
            anywhere,
            anywhere,
            smem,
            anywhere,
            vmem,
            vmem,
            vmem,
            vmem,
            anywhere,
            anywhere,
            anywhere,
        ],
        out_specs=vmem,
        scratch_shapes=scratch,
        compiler_params=pltpu.CompilerParams(
            collective_id=0, has_side_effects=True, vmem_limit_bytes=60 * 1024 * 1024
        ),
    )(
        query,
        cache_keys,
        cache_values,
        lengths,
        out_proj,
        residual,
        norm_gain,
        router.T,
        expert_ids.transpose(0, 2, 1),
        gate_weight,
        up_weight,
        down_weight,
    )


def solution(mesh):
    in_specs = (
        P(None, ("req", "exp"), "head"),
        P(None, ("req", "exp"), None, "head"),
        P(None, ("req", "exp"), None, "head"),
        P(None, ("req", "exp")),
        P("head", "exp"),
        P(None, ("req", "head"), "exp"),
        P("exp"),
        P("exp", None),
        P(None, ("req", "head"), None),
        P("exp", None, ("req", "head")),
        P("exp", None, ("req", "head")),
        P("exp", "req", "head"),
    )
    out_specs = P(None, ("req", "head"), "exp")
    return jax.shard_map(
        functools.partial(per_device, mesh.shape["exp"]),
        mesh=mesh,
        in_specs=in_specs,
        out_specs=out_specs,
        check_vma=False,
    )
```

```python
import functools

import jax
import jax.numpy as jnp
from jax import lax
from jax.experimental import pallas as pl
from jax.experimental.pallas import tpu as pltpu
from jax.sharding import PartitionSpec as P

MESH = pl.DeviceIdType.MESH
HEAD_DIM = 128
SLOTS = 4
F32 = jnp.float32
BF16 = jnp.bfloat16
EXACT = lax.Precision.HIGHEST


def iota(shape, axis):
    return lax.broadcasted_iota(jnp.int32, shape, axis)


def dot(a, b, **kw):
    return jnp.dot(a, b, preferred_element_type=F32, **kw)


def dot_t(a, b, **kw):
    return lax.dot_general(a, b, (((1,), (1,)), ((), ())), preferred_element_type=F32, **kw)


class Swap:
    def __init__(self, axis, me, n, src, dst, sems):
        self.axis, self.me, self.n, self.src, self.dst = axis, me, n, src, dst
        self.sems = sems

    def copy(self, d, to, at):
        return pltpu.make_async_remote_copy(
            src_ref=self.src(to),
            dst_ref=self.dst(at),
            send_sem=self.sems.at[0, d - 1],
            recv_sem=self.sems.at[1, d - 1],
            device_id={self.axis: to},
            device_id_type=MESH,
        )

    def start(self):
        for d in range(1, self.n):
            self.copy(d, lax.rem(self.me + d, self.n), self.me).start()

    def wait_recv(self):
        for d in range(1, self.n):
            source = lax.rem(self.me + self.n - d, self.n)
            self.copy(d, source, source).wait_recv()

    def wait_send(self):
        for d in range(1, self.n):
            self.copy(d, lax.rem(self.me + d, self.n), self.me).wait_send()


class Ring:
    def __init__(self, axis, me, n, block_ref, sems):
        self.axis, self.me, self.n, self.block_ref, self.sems = axis, me, n, block_ref, sems
        self.half = n // 2

    def block(self, way, k):
        return lax.rem(self.me + (self.n - k if way == 0 else k), self.n)

    def copy(self, way, k, block):
        ref = self.block_ref(block)
        if k == self.half:
            rows = ref.shape[0] // 2
            ref = ref.at[pl.ds(way * rows, rows)]
        to = lax.rem(self.me + (1 if way == 0 else self.n - 1), self.n)
        return pltpu.make_async_remote_copy(
            src_ref=ref,
            dst_ref=ref,
            send_sem=self.sems.at[2 * way, k - 1],
            recv_sem=self.sems.at[2 * way + 1, k - 1],
            device_id={self.axis: to},
            device_id_type=MESH,
        )

    def send(self, way, k):
        self.copy(way, k, self.block(way, k - 1)).start()

    def start(self):
        for way in (0, 1):
            self.send(way, 1)

    def step(self, k):
        for way in (0, 1):
            self.copy(way, k, self.block(way, k)).wait_recv()
            if k < self.half:
                self.send(way, k + 1)

    def blocks(self, k):
        return [self.block(way, k) for way in ((0, 1) if k < self.half else (0,))]

    def wait_send(self):
        for k in range(1, self.half + 1):
            for way in (0, 1):
                self.copy(way, k, self.block(way, k - 1)).wait_send()


def layer(
    n,
    query_ref,
    keys_hbm,
    values_hbm,
    lengths_ref,
    proj_hbm,
    residual_ref,
    gain_ref,
    router_ref,
    ids_ref,
    gate_hbm,
    up_hbm,
    down_hbm,
    out_ref,
    keys,
    values,
    proj,
    wide,
    down,
    aux_all,
    att_all,
    part_own,
    part_send,
    part_recv,
    stream_all,
    first_a,
    first_b,
    rows_a,
    rows_b,
    hidden,
    acc,
    down_send,
    down_recv,
    back_send,
    back_recv,
    load_sem,
    swap_sem,
    ring_sem,
    back_sem,
):
    micro, group, width = query_ref.shape
    tokens = micro * group
    slots = micro * SLOTS
    r, h, e = lax.axis_index("req"), lax.axis_index("head"), lax.axis_index("exp")
    features = n * width
    hidden_width = gate_hbm.shape[2]
    positions = keys_hbm.shape[2]

    barrier = pltpu.get_barrier_semaphore()
    for axis, me in (("exp", e), ("head", h), ("req", r)):
        for d in range(1, n):
            pl.semaphore_signal(
                barrier, inc=1, device_id={axis: lax.rem(me + d, n)}, device_id_type=MESH
            )
    for j in range(n):

        @pl.when(jnp.logical_or(h != e, e != j))
        def _():
            pl.semaphore_signal(
                barrier, inc=1, device_id={"head": e, "exp": jnp.int32(j)}, device_id_type=MESH
            )

    loads = [
        pltpu.make_async_copy(keys_hbm, keys, load_sem.at[0]),
        pltpu.make_async_copy(values_hbm, values, load_sem.at[1]),
        pltpu.make_async_copy(proj_hbm, proj, load_sem.at[2]),
        pltpu.make_async_copy(gate_hbm.at[0], wide.at[:, pl.ds(0, hidden_width)], load_sem.at[3]),
        pltpu.make_async_copy(
            up_hbm.at[0], wide.at[:, pl.ds(hidden_width, hidden_width)], load_sem.at[4]
        ),
        pltpu.make_async_copy(down_hbm.at[0], down, load_sem.at[5]),
    ]
    for load in loads:
        load.start()

    per_key = width // HEAD_DIM
    queries = query_ref[...].astype(F32).reshape(tokens, width)
    queries = jnp.concatenate(
        [queries[:, j * HEAD_DIM : (j + 1) * HEAD_DIM] for j in range(per_key)], axis=0
    ).astype(BF16)
    columns = tokens * positions
    owner = iota((1, columns), 1) // positions
    limit = jnp.zeros((1, columns), jnp.int32)
    for t in range(tokens):
        limit = jnp.where(owner == t, lengths_ref[t // group, t % group], limit)
    valid = lax.rem(iota((1, columns), 1), positions) < limit
    owner = jnp.where(valid, owner, -1)
    allowed = lax.rem(iota((per_key * tokens, columns), 0), tokens) == owner
    loads[0].wait()
    scores = dot_t(queries, keys[...].reshape(columns, HEAD_DIM)) * HEAD_DIM ** (-0.5)
    scores = jnp.where(allowed, scores, F32(-1e30))
    exponents = jnp.exp(scores - jnp.max(scores, axis=-1, keepdims=True))
    weights = (exponents / jnp.sum(exponents, axis=-1, keepdims=True)).astype(BF16)
    loads[1].wait()
    mixed = dot(weights, values[...].reshape(columns, HEAD_DIM))
    for j in range(per_key):
        att_all[e, :, j * HEAD_DIM : (j + 1) * HEAD_DIM] = mixed[
            j * tokens : (j + 1) * tokens
        ].astype(BF16)
    gain = jnp.broadcast_to(gain_ref[...].astype(F32).reshape(1, width), (n, width))
    aux_all[e] = jnp.concatenate([router_ref[...].astype(F32), gain], axis=0).astype(BF16)

    pl.semaphore_wait(barrier, 3 * (n - 1) + n - jnp.where(h == e, 1, 0))

    swap_att = Swap("exp", e, n, lambda to: att_all.at[e], lambda at: att_all.at[at], swap_sem.at[0])
    swap_aux = Swap("exp", e, n, lambda to: aux_all.at[e], lambda at: aux_all.at[at], swap_sem.at[1])
    swap_att.start()
    swap_aux.start()

    places = n * slots
    diagonal = iota((group, group), 0) == iota((group, group), 1)

    def upright(row):
        return jnp.sum(jnp.where(diagonal, row, F32(0.0)), axis=-1, keepdims=True)

    ids = [
        jnp.concatenate(
            [upright(ids_ref[m][k : k + 1, :].astype(F32)) for m in range(micro)], axis=0
        ).astype(jnp.int32)
        for k in range(2)
    ]
    token_at = iota((tokens, places), 0)
    column = iota((tokens, places), 1)
    hots = [(ids[k] == column // slots).astype(F32) for k in range(2)]
    earlier_of = (
        (iota((tokens, tokens), 1) < iota((tokens, tokens), 0))
        & (iota((tokens, tokens), 1) // group == iota((tokens, tokens), 0) // group)
    ).astype(BF16)
    earlier = dot(earlier_of, (hots[0] + hots[1]).astype(BF16))
    fits = (lax.rem(column, SLOTS).astype(F32) == earlier) & (
        lax.rem(column, slots) // SLOTS == token_at // group
    )
    chosen_at = [jnp.where(fits, hot, F32(0.0)) for hot in hots]
    sel_own = dot_t(
        ((iota((slots, places), 1) - slots * e) == iota((slots, places), 0)).astype(BF16),
        (chosen_at[0] + chosen_at[1]).astype(BF16),
    ).astype(BF16)

    loads[2].wait()
    swap_att.wait_recv()
    partial = dot(att_all[...].reshape(n * tokens, width), proj[...]).reshape(n, tokens, width)
    part_own[...] = partial
    part_send[...] = partial.astype(BF16)
    swap_part = Swap(
        "head", h, n, lambda to: part_send.at[to], lambda at: part_recv.at[at], swap_sem.at[2]
    )
    swap_part.start()
    projected = part_own[h]
    residual = residual_ref[...].astype(F32).reshape(tokens, width)
    swap_part.wait_recv()
    for d in range(1, n):
        projected += part_recv[lax.rem(h + d, n)].astype(F32)
    stream_all[e] = (residual + projected).astype(BF16)
    swap_stream = Swap(
        "exp", e, n, lambda to: stream_all.at[e], lambda at: stream_all.at[at], swap_sem.at[3]
    )
    swap_stream.start()
    swap_aux.wait_recv()
    swap_stream.wait_recv()

    squares = jnp.zeros((tokens, width), F32)
    for j in range(n):
        block = stream_all[j].astype(F32)
        squares += block * block
    inverse = lax.rsqrt(jnp.sum(squares, axis=-1, keepdims=True) / features + 1e-05)
    normed = []
    for j in range(n):
        full = stream_all[j].astype(F32) * aux_all[j].astype(F32)[n : n + 1] * inverse
        normed.append(full)
    chunks = n // 2
    packed = chunks * SLOTS
    stacked = [
        jnp.concatenate([full.astype(BF16) for full in normed[i * chunks : (i + 1) * chunks]], axis=0)
        for i in range(2)
    ]
    first_swaps = []
    for m in range(micro):
        pick = (
            iota((packed, slots), 1) == m * SLOTS + lax.rem(iota((packed, slots), 0), SLOTS)
        ).astype(BF16)
        spread = (
            lax.rem(iota((tokens, chunks * tokens), 1), tokens)
            == iota((tokens, chunks * tokens), 0)
        ).astype(BF16)
        same = (
            iota((packed, chunks * tokens), 0) // SLOTS
            == iota((packed, chunks * tokens), 1) // tokens
        )
        take = dot(dot(pick, sel_own).astype(BF16), spread)
        take = jnp.where(same, take, F32(0.0)).astype(BF16)
        first_a[m, h] = dot(take, stacked[0]).astype(BF16)
        first_b[m, r] = dot(take, stacked[1]).astype(BF16)
        swap_a = Swap(
            "head",
            h,
            n,
            lambda to, m=m: first_a.at[m, h],
            lambda at, m=m: first_a.at[m, at],
            swap_sem.at[4 + 2 * m],
        )
        swap_b = Swap(
            "req",
            r,
            n,
            lambda to, m=m: first_b.at[m, r],
            lambda at, m=m: first_b.at[m, at],
            swap_sem.at[5 + 2 * m],
        )
        swap_a.start()
        swap_b.start()
        first_swaps.append((swap_a, swap_b))

    half = features // 2
    block_rows = n * SLOTS
    all_rows = n * block_rows
    ordered = iota((n * packed, n * packed), 0)
    ordered = (
        lax.rem(ordered, block_rows) // SLOTS * packed
        + ordered // block_rows * SLOTS
        + lax.rem(ordered, SLOTS)
        == iota((n * packed, n * packed), 1)
    ).astype(BF16)

    def settle(first, rows_to):
        y = dot(ordered, first[...].reshape(n * packed, width)).astype(BF16)
        for c in range(chunks):
            rows_to[:, pl.ds(c * width, width)] = y[c * block_rows : (c + 1) * block_rows]

    rings_a = [
        Ring("req", r, n, lambda b, m=m: rows_a.at[b, m], ring_sem.at[m]) for m in range(micro)
    ]
    rings_b = [
        Ring("head", h, n, lambda b, m=m: rows_b.at[b, m], ring_sem.at[micro + m])
        for m in range(micro)
    ]
    rings_h = [
        Ring("head", h, n, lambda b, m=m: hidden.at[b, m], ring_sem.at[2 * micro + m])
        for m in range(micro)
    ]

    def settle_a(m):
        first_swaps[m][0].wait_recv()
        settle(first_a.at[m], rows_a.at[r, m])

    def settle_b(m):
        first_swaps[m][1].wait_recv()
        settle(first_b.at[m], rows_b.at[h, m])

    settle_a(0)
    rings_a[0].start()
    settle_b(0)
    rings_b[0].start()
    settle_a(1)
    settle_b(1)

    logits = jnp.zeros((tokens, 2 * n), F32)
    for j in range(n):
        logits += dot_t(normed[j], aux_all[j].astype(F32), precision=EXACT)
    lane = iota((tokens, 2 * n), 1)
    powers = [
        jnp.exp(jnp.sum(jnp.where(lane == ids[k], logits, F32(0.0)), axis=-1, keepdims=True))
        for k in range(2)
    ]
    total = powers[0] + powers[1]
    mixing = powers[0] / total * chosen_at[0] + powers[1] / total * chosen_at[1]

    crossed = iota((all_rows, all_rows), 0)
    crossed = (
        lax.rem(crossed, block_rows) // SLOTS * block_rows
        + crossed // block_rows * SLOTS
        + lax.rem(crossed, SLOTS)
        == iota((all_rows, all_rows), 1)
    ).astype(BF16)

    def activate(m):
        x = rows_a[:, m].reshape(all_rows, half)
        y = dot(x, wide[pl.ds(0, half), :])
        x = dot(crossed, rows_b[:, m].reshape(all_rows, half)).astype(BF16)
        y += dot(x, wide[pl.ds(half, half), :])
        gated, upward = y[:, :hidden_width], y[:, hidden_width:]
        hidden[h, m] = (gated / (1.0 + jnp.exp(-gated)) * upward).astype(BF16)
        rings_h[m].start()

    def lower(b, m, first=False):
        y = dot(
            hidden[b, m], down[pl.ds(pl.multiple_of(b * hidden_width, hidden_width), hidden_width), :]
        ).reshape(n, block_rows, width)
        acc[m] = y if first else acc[m] + y

    def gather_step(m, k):
        rings_a[m].step(k)
        rings_b[m].step(k)

    def hidden_step(m, k):
        rings_h[m].step(k)
        for b in rings_h[m].blocks(k):
            lower(b, m)

    swaps_down = [
        Swap(
            "req",
            r,
            n,
            lambda to, m=m: down_send.at[m, to],
            lambda at, m=m: down_recv.at[m, at],
            swap_sem.at[8 + m],
        )
        for m in range(micro)
    ]

    def hand_over(m):
        down_send[m] = acc[m].astype(BF16)
        swaps_down[m].start()

    def collect(m):
        total = acc[m, r]
        swaps_down[m].wait_recv()
        for d in range(1, n):
            total += down_recv[m, lax.rem(r + d, n)].astype(F32)
        return total.astype(BF16)

    gather_step(0, 1)
    rings_a[1].start()
    rings_b[1].start()
    loads[3].wait()
    loads[4].wait()
    loads[5].wait()
    gather_step(0, 2)
    gather_step(1, 1)
    gather_step(0, 3)
    gather_step(1, 2)
    gather_step(0, 4)
    activate(0)
    gather_step(1, 3)
    gather_step(1, 4)
    lower(h, 0, True)
    hidden_step(0, 1)
    activate(1)
    hidden_step(0, 2)
    lower(h, 1, True)
    hidden_step(1, 1)
    hidden_step(0, 3)
    hidden_step(1, 2)
    hidden_step(0, 4)
    hand_over(0)
    hidden_step(1, 3)
    hidden_step(1, 4)
    hand_over(1)

    expert_rows = jnp.concatenate([collect(m) for m in range(micro)], axis=0)
    sorted_rows = iota((micro * block_rows, micro * block_rows), 0)
    sorted_rows = (
        lax.rem(sorted_rows, slots) // SLOTS * block_rows
        + sorted_rows // slots * SLOTS
        + lax.rem(sorted_rows, SLOTS)
        == iota((micro * block_rows, micro * block_rows), 1)
    ).astype(BF16)
    back_send[...] = dot(sorted_rows, expert_rows).reshape(n, slots, width)

    def back(to, at):
        return pltpu.make_async_remote_copy(
            src_ref=back_send.at[to],
            dst_ref=back_recv.at[at],
            send_sem=back_sem.at[0, to],
            recv_sem=back_sem.at[1, at],
            device_id={"head": jnp.int32(to), "exp": h},
            device_id_type=MESH,
        )

    for j in range(n):

        @pl.when(jnp.logical_or(h != e, h != j))
        def _():
            back(j, e).start()

        @pl.when(jnp.logical_and(h == e, h == j))
        def _():
            back_recv[j] = back_send[j]

    for j in range(n):

        @pl.when(jnp.logical_or(h != e, e != j))
        def _():
            back(j, j).wait_recv()

    returned = back_recv[...].reshape(places, width)
    result = stream_all[e].astype(F32) + dot(mixing, returned, precision=EXACT)
    out_ref[...] = result.reshape(micro, group, width).astype(BF16)

    swaps = [swap_att, swap_aux, swap_part, swap_stream, *swaps_down]
    for pair in first_swaps:
        swaps += pair
    for swap in swaps:
        swap.wait_send()
    for ring in rings_a + rings_b + rings_h:
        ring.wait_send()
    for j in range(n):

        @pl.when(jnp.logical_or(h != e, h != j))
        def _():
            back(j, e).wait_send()


def per_device(
    n,
    query,
    cache_keys,
    cache_values,
    lengths,
    out_proj,
    residual,
    norm_gain,
    router,
    expert_ids,
    gate_weight,
    up_weight,
    down_weight,
):
    micro, group, width = query.shape
    tokens, slots = micro * group, micro * SLOTS
    features = n * width
    hidden_width = gate_weight.shape[2]
    vmem = pl.BlockSpec(memory_space=pltpu.VMEM)
    smem = pl.BlockSpec(memory_space=pltpu.SMEM)
    anywhere = pl.BlockSpec(memory_space=pl.ANY)

    block_rows = n * SLOTS
    all_rows = n * block_rows
    scratch = [
        pltpu.VMEM(cache_keys.shape, BF16),
        pltpu.VMEM(cache_values.shape, BF16),
        pltpu.VMEM(out_proj.shape, BF16),
        pltpu.VMEM((features, 2 * hidden_width), BF16),
        pltpu.VMEM(down_weight.shape[1:], BF16),
        pltpu.VMEM((n, 2 * n, width), BF16),
        pltpu.VMEM((n, tokens, width), BF16),
        pltpu.VMEM((n, tokens, width), F32),
        pltpu.VMEM((n, tokens, width), BF16),
        pltpu.VMEM((n, tokens, width), BF16),
        pltpu.VMEM((n, tokens, width), BF16),
        pltpu.VMEM((micro, n, n // 2 * SLOTS, width), BF16),
        pltpu.VMEM((micro, n, n // 2 * SLOTS, width), BF16),
        pltpu.VMEM((n, micro, block_rows, features // 2), BF16),
        pltpu.VMEM((n, micro, block_rows, features // 2), BF16),
        pltpu.VMEM((n, micro, all_rows, hidden_width), BF16),
        pltpu.VMEM((micro, n, block_rows, width), F32),
        pltpu.VMEM((micro, n, block_rows, width), BF16),
        pltpu.VMEM((micro, n, block_rows, width), BF16),
        pltpu.VMEM((n, slots, width), F32),
        pltpu.VMEM((n, slots, width), F32),
        pltpu.SemaphoreType.DMA((6,)),
        pltpu.SemaphoreType.DMA((10, 2, n - 1)),
        pltpu.SemaphoreType.DMA((3 * micro, 4, n // 2)),
        pltpu.SemaphoreType.DMA((2, n)),
    ]
    return pl.pallas_call(
        functools.partial(layer, n),
        out_shape=jax.ShapeDtypeStruct((micro, group, width), BF16),
        in_specs=[
            vmem,
            anywhere,
            anywhere,
            smem,
            anywhere,
            vmem,
            vmem,
            vmem,
            vmem,
            anywhere,
            anywhere,
            anywhere,
        ],
        out_specs=vmem,
        scratch_shapes=scratch,
        compiler_params=pltpu.CompilerParams(
            collective_id=0, has_side_effects=True, vmem_limit_bytes=60 * 1024 * 1024
        ),
    )(
        query,
        cache_keys,
        cache_values,
        lengths,
        out_proj,
        residual,
        norm_gain,
        router.T,
        expert_ids.transpose(0, 2, 1),
        gate_weight,
        up_weight,
        down_weight,
    )


def solution(mesh):
    in_specs = (
        P(None, ("req", "exp"), "head"),
        P(None, ("req", "exp"), None, "head"),
        P(None, ("req", "exp"), None, "head"),
        P(None, ("req", "exp")),
        P("head", "exp"),
        P(None, ("req", "head"), "exp"),
        P("exp"),
        P("exp", None),
        P(None, ("req", "head"), None),
        P("exp", None, ("req", "head")),
        P("exp", None, ("req", "head")),
        P("exp", "req", "head"),
    )
    out_specs = P(None, ("req", "head"), "exp")
    return jax.shard_map(
        functools.partial(per_device, mesh.shape["exp"]),
        mesh=mesh,
        in_specs=in_specs,
        out_specs=out_specs,
        check_vma=False,
    )
```

```python
import functools

import jax
import jax.numpy as jnp
from jax import lax
from jax.experimental import pallas as pl
from jax.experimental.pallas import tpu as pltpu
from jax.sharding import PartitionSpec as P

MESH = pl.DeviceIdType.MESH
HEAD_DIM = 128
SLOTS = 4
F32 = jnp.float32
BF16 = jnp.bfloat16


def iota(shape, axis):
    return lax.broadcasted_iota(jnp.int32, shape, axis)


def dot(a, b, **kw):
    return jnp.dot(a, b, preferred_element_type=F32, **kw)


def dot_t(a, b, **kw):
    return lax.dot_general(a, b, (((1,), (1,)), ((), ())), preferred_element_type=F32, **kw)


def pieces(x):
    high = x.astype(BF16)
    rest = x - high.astype(F32)
    middle = rest.astype(BF16)
    return high, middle, (rest - middle.astype(F32)).astype(BF16)


class Swap:
    def __init__(self, axis, me, n, src, dst, sems):
        self.axis, self.me, self.n, self.src, self.dst = axis, me, n, src, dst
        self.sems = sems

    def copy(self, d, to, at):
        return pltpu.make_async_remote_copy(
            src_ref=self.src(to),
            dst_ref=self.dst(at),
            send_sem=self.sems.at[0, d - 1],
            recv_sem=self.sems.at[1, d - 1],
            device_id={self.axis: to},
            device_id_type=MESH,
        )

    def start(self):
        for d in range(1, self.n):
            self.copy(d, lax.rem(self.me + d, self.n), self.me).start()

    def wait_recv(self):
        for d in range(1, self.n):
            source = lax.rem(self.me + self.n - d, self.n)
            self.copy(d, source, source).wait_recv()

    def wait_send(self):
        for d in range(1, self.n):
            self.copy(d, lax.rem(self.me + d, self.n), self.me).wait_send()


class Ring:
    def __init__(self, axis, me, n, block_ref, sems):
        self.axis, self.me, self.n, self.block_ref, self.sems = axis, me, n, block_ref, sems
        self.half = n // 2

    def block(self, way, k):
        return lax.rem(self.me + (self.n - k if way == 0 else k), self.n)

    def copy(self, way, k, block):
        ref = self.block_ref(block)
        if k == self.half:
            rows = ref.shape[0] // 2
            ref = ref.at[pl.ds(way * rows, rows)]
        to = lax.rem(self.me + (1 if way == 0 else self.n - 1), self.n)
        return pltpu.make_async_remote_copy(
            src_ref=ref,
            dst_ref=ref,
            send_sem=self.sems.at[2 * way, k - 1],
            recv_sem=self.sems.at[2 * way + 1, k - 1],
            device_id={self.axis: to},
            device_id_type=MESH,
        )

    def send(self, way, k):
        self.copy(way, k, self.block(way, k - 1)).start()

    def start(self):
        for way in (0, 1):
            self.send(way, 1)

    def step(self, k):
        for way in (0, 1):
            self.copy(way, k, self.block(way, k)).wait_recv()
            if k < self.half:
                self.send(way, k + 1)

    def blocks(self, k):
        return [self.block(way, k) for way in ((0, 1) if k < self.half else (0,))]

    def wait_send(self):
        for k in range(1, self.half + 1):
            for way in (0, 1):
                self.copy(way, k, self.block(way, k - 1)).wait_send()


def layer(
    n,
    query_ref,
    keys_hbm,
    values_hbm,
    lengths_ref,
    proj_hbm,
    residual_ref,
    gain_ref,
    router_ref,
    ids_ref,
    gate_hbm,
    up_hbm,
    down_hbm,
    out_ref,
    keys,
    values,
    proj,
    wide,
    down,
    aux_all,
    att_all,
    part_own,
    part_send,
    part_recv,
    stream_all,
    first_a,
    first_b,
    rows_a,
    rows_b,
    take_all,
    ordered,
    crossed,
    sorted_rows,
    hidden,
    acc,
    down_send,
    down_recv,
    back_send,
    back_recv,
    load_sem,
    swap_sem,
    ring_sem,
    back_sem,
):
    micro, group, width = query_ref.shape
    tokens = micro * group
    slots = micro * SLOTS
    r, h, e = lax.axis_index("req"), lax.axis_index("head"), lax.axis_index("exp")
    features = n * width
    hidden_width = gate_hbm.shape[2]
    positions = keys_hbm.shape[2]

    barrier = pltpu.get_barrier_semaphore()
    for axis, me in (("exp", e), ("head", h), ("req", r)):
        for d in range(1, n):
            pl.semaphore_signal(
                barrier, inc=1, device_id={axis: lax.rem(me + d, n)}, device_id_type=MESH
            )
    for j in range(n):

        @pl.when(jnp.logical_or(h != e, e != j))
        def _():
            pl.semaphore_signal(
                barrier, inc=1, device_id={"head": e, "exp": jnp.int32(j)}, device_id_type=MESH
            )

    loads = [
        pltpu.make_async_copy(keys_hbm, keys, load_sem.at[0]),
        pltpu.make_async_copy(values_hbm, values, load_sem.at[1]),
        pltpu.make_async_copy(proj_hbm, proj, load_sem.at[2]),
        pltpu.make_async_copy(gate_hbm.at[0], wide.at[:, pl.ds(0, hidden_width)], load_sem.at[3]),
        pltpu.make_async_copy(
            up_hbm.at[0], wide.at[:, pl.ds(hidden_width, hidden_width)], load_sem.at[4]
        ),
        pltpu.make_async_copy(down_hbm.at[0], down, load_sem.at[5]),
    ]
    for load in loads:
        load.start()

    with jax.named_scope("attention"):
        per_key = width // HEAD_DIM
        queries = query_ref[...].astype(F32).reshape(tokens, width)
        queries = jnp.concatenate(
            [queries[:, j * HEAD_DIM : (j + 1) * HEAD_DIM] for j in range(per_key)], axis=0
        ).astype(BF16)
        columns = tokens * positions
        owner = iota((1, columns), 1) // positions
        limit = jnp.zeros((1, columns), jnp.int32)
        for t in range(tokens):
            limit = jnp.where(owner == t, lengths_ref[t // group, t % group], limit)
        valid = lax.rem(iota((1, columns), 1), positions) < limit
        owner = jnp.where(valid, owner, -1)
        allowed = lax.rem(iota((per_key * tokens, columns), 0), tokens) == owner
        loads[0].wait()
        scores = dot_t(queries, keys[...].reshape(columns, HEAD_DIM)) * HEAD_DIM ** (-0.5)
        scores = jnp.where(allowed, scores, F32(-1e30))
        exponents = jnp.exp(scores - jnp.max(scores, axis=-1, keepdims=True))
        weights = (exponents / jnp.sum(exponents, axis=-1, keepdims=True)).astype(BF16)
        loads[1].wait()
        mixed = dot(weights, values[...].reshape(columns, HEAD_DIM))
        for j in range(per_key):
            att_all[e, :, j * HEAD_DIM : (j + 1) * HEAD_DIM] = mixed[
                j * tokens : (j + 1) * tokens
            ].astype(BF16)
        gain = jnp.broadcast_to(gain_ref[...].astype(F32).reshape(1, width), (n, width))
        aux_all[e] = jnp.concatenate([router_ref[...].astype(F32), gain], axis=0).astype(BF16)

    with jax.named_scope("entry"):
        pl.semaphore_wait(barrier, 3 * (n - 1) + n - jnp.where(h == e, 1, 0))

    swap_att = Swap("exp", e, n, lambda to: att_all.at[e], lambda at: att_all.at[at], swap_sem.at[0])
    swap_aux = Swap("exp", e, n, lambda to: aux_all.at[e], lambda at: aux_all.at[at], swap_sem.at[1])
    swap_att.start()
    swap_aux.start()

    with jax.named_scope("routing"):
        places = n * slots
        diagonal = iota((group, group), 0) == iota((group, group), 1)

        def upright(row):
            return jnp.sum(jnp.where(diagonal, row, F32(0.0)), axis=-1, keepdims=True)

        ids = [
            jnp.concatenate(
                [upright(ids_ref[m][k : k + 1, :].astype(F32)) for m in range(micro)], axis=0
            ).astype(jnp.int32)
            for k in range(2)
        ]
        token_at = iota((tokens, places), 0)
        column = iota((tokens, places), 1)
        hots = [(ids[k] == column // slots).astype(F32) for k in range(2)]
        earlier_of = (
            (iota((tokens, tokens), 1) < iota((tokens, tokens), 0))
            & (iota((tokens, tokens), 1) // group == iota((tokens, tokens), 0) // group)
        ).astype(BF16)
        earlier = dot(earlier_of, (hots[0] + hots[1]).astype(BF16))
        fits = (lax.rem(column, SLOTS).astype(F32) == earlier) & (
            lax.rem(column, slots) // SLOTS == token_at // group
        )
        chosen_at = [jnp.where(fits, hot, F32(0.0)) for hot in hots]
        sel_own = dot_t(
            ((iota((slots, places), 1) - slots * e) == iota((slots, places), 0)).astype(BF16),
            (chosen_at[0] + chosen_at[1]).astype(BF16),
        ).astype(BF16)

        chunks = n // 2
        packed = chunks * SLOTS
        block_rows = n * SLOTS
        all_rows = n * block_rows
        for m in range(micro):
            pick = (
                iota((packed, slots), 1) == m * SLOTS + lax.rem(iota((packed, slots), 0), SLOTS)
            ).astype(BF16)
            spread = (
                lax.rem(iota((tokens, chunks * tokens), 1), tokens)
                == iota((tokens, chunks * tokens), 0)
            ).astype(BF16)
            same = (
                iota((packed, chunks * tokens), 0) // SLOTS
                == iota((packed, chunks * tokens), 1) // tokens
            )
            take = dot(dot(pick, sel_own).astype(BF16), spread)
            take_all[m] = jnp.where(same, take, F32(0.0)).astype(BF16)

        def one_hot(size, place):
            return (place(iota((size, size), 0)) == iota((size, size), 1)).astype(BF16)

        ordered[...] = one_hot(
            n * packed,
            lambda i: lax.rem(i, block_rows) // SLOTS * packed
            + i // block_rows * SLOTS
            + lax.rem(i, SLOTS),
        )
        crossed[...] = one_hot(
            all_rows,
            lambda i: lax.rem(i, block_rows) // SLOTS * block_rows
            + i // block_rows * SLOTS
            + lax.rem(i, SLOTS),
        )
        sorted_rows[...] = one_hot(
            micro * block_rows,
            lambda i: lax.rem(i, slots) // SLOTS * block_rows + i // slots * SLOTS + lax.rem(i, SLOTS),
        )

    with jax.named_scope("projection"):
        loads[2].wait()
        swap_att.wait_recv()
        partial = dot(att_all[...].reshape(n * tokens, width), proj[...]).reshape(n, tokens, width)
        part_own[...] = partial
        part_send[...] = partial.astype(BF16)
        swap_part = Swap(
            "head", h, n, lambda to: part_send.at[to], lambda at: part_recv.at[at], swap_sem.at[2]
        )
        swap_part.start()
    with jax.named_scope("stream"):
        projected = part_own[h]
        residual = residual_ref[...].astype(F32).reshape(tokens, width)
        swap_part.wait_recv()
        for d in range(1, n):
            projected += part_recv[lax.rem(h + d, n)].astype(F32)
        stream_all[e] = (residual + projected).astype(BF16)
        swap_stream = Swap(
            "exp", e, n, lambda to: stream_all.at[e], lambda at: stream_all.at[at], swap_sem.at[3]
        )
        swap_stream.start()
    with jax.named_scope("norm"):
        swap_aux.wait_recv()
        swap_stream.wait_recv()

        squares = jnp.zeros((tokens, width), F32)
        for j in range(n):
            block = stream_all[j].astype(F32)
            squares += block * block
        inverse = lax.rsqrt(jnp.sum(squares, axis=-1, keepdims=True) / features + 1e-05)
        normed = []
        for j in range(n):
            full = stream_all[j].astype(F32) * aux_all[j].astype(F32)[n : n + 1] * inverse
            normed.append(full)
        stacked = [
            jnp.concatenate([full.astype(BF16) for full in normed[i * chunks : (i + 1) * chunks]], axis=0)
            for i in range(2)
        ]
        first_swaps = []
        for m in range(micro):
            take = take_all[m]
            first_a[m, h] = dot(take, stacked[0]).astype(BF16)
            first_b[m, r] = dot(take, stacked[1]).astype(BF16)
            swap_a = Swap(
                "head",
                h,
                n,
                lambda to, m=m: first_a.at[m, h],
                lambda at, m=m: first_a.at[m, at],
                swap_sem.at[4 + 2 * m],
            )
            swap_b = Swap(
                "req",
                r,
                n,
                lambda to, m=m: first_b.at[m, r],
                lambda at, m=m: first_b.at[m, at],
                swap_sem.at[5 + 2 * m],
            )
            swap_a.start()
            swap_b.start()
            first_swaps.append((swap_a, swap_b))

    half = features // 2

    def settle(first, rows_to):
        y = dot(ordered[...], first[...].reshape(n * packed, width)).astype(BF16)
        for c in range(chunks):
            rows_to[:, pl.ds(c * width, width)] = y[c * block_rows : (c + 1) * block_rows]

    rings_a = [
        Ring("req", r, n, lambda b, m=m: rows_a.at[b, m], ring_sem.at[m]) for m in range(micro)
    ]
    rings_b = [
        Ring("head", h, n, lambda b, m=m: rows_b.at[b, m], ring_sem.at[micro + m])
        for m in range(micro)
    ]
    rings_h = [
        Ring("head", h, n, lambda b, m=m: hidden.at[b, m], ring_sem.at[2 * micro + m])
        for m in range(micro)
    ]

    def settle_a(m):
        first_swaps[m][0].wait_recv()
        settle(first_a.at[m], rows_a.at[r, m])

    def settle_b(m):
        first_swaps[m][1].wait_recv()
        settle(first_b.at[m], rows_b.at[h, m])

    with jax.named_scope("settle"):
        settle_a(0)
        rings_a[0].start()
        settle_b(0)
        rings_b[0].start()
        settle_a(1)
        settle_b(1)

    def mix():
        logits = jnp.zeros((tokens, 2 * n), F32)
        for j in range(n):
            full = stream_all[j].astype(F32) * aux_all[j].astype(F32)[n : n + 1] * inverse
            for piece in pieces(full):
                logits += dot_t(piece, aux_all[j])
        lane = iota((tokens, 2 * n), 1)
        powers = [
            jnp.exp(jnp.sum(jnp.where(lane == ids[k], logits, F32(0.0)), axis=-1, keepdims=True))
            for k in range(2)
        ]
        total = powers[0] + powers[1]
        return powers[0] / total * chosen_at[0] + powers[1] / total * chosen_at[1]

    def activate(m):
        x = rows_a[:, m].reshape(all_rows, half)
        y = dot(x, wide[pl.ds(0, half), :])
        x = dot(crossed[...], rows_b[:, m].reshape(all_rows, half)).astype(BF16)
        y += dot(x, wide[pl.ds(half, half), :])
        gated, upward = y[:, :hidden_width], y[:, hidden_width:]
        hidden[h, m] = (gated / (1.0 + jnp.exp(-gated)) * upward).astype(BF16)
        rings_h[m].start()

    def lower(b, m, first=False):
        y = dot(
            hidden[b, m], down[pl.ds(pl.multiple_of(b * hidden_width, hidden_width), hidden_width), :]
        ).reshape(n, block_rows, width)
        acc[m] = y if first else acc[m] + y

    def gather_step(m, k):
        rings_a[m].step(k)
        rings_b[m].step(k)

    def hidden_step(m, k):
        rings_h[m].step(k)
        for b in rings_h[m].blocks(k):
            lower(b, m)

    swaps_down = [
        Swap(
            "req",
            r,
            n,
            lambda to, m=m: down_send.at[m, to],
            lambda at, m=m: down_recv.at[m, at],
            swap_sem.at[8 + m],
        )
        for m in range(micro)
    ]

    def hand_over(m):
        down_send[m] = acc[m].astype(BF16)
        swaps_down[m].start()

    def collect(m):
        total = acc[m, r]
        swaps_down[m].wait_recv()
        for d in range(1, n):
            total += down_recv[m, lax.rem(r + d, n)].astype(F32)
        return total.astype(BF16)

    with jax.named_scope("rows_first"):
        gather_step(0, 1)
        rings_a[1].start()
        rings_b[1].start()
        loads[3].wait()
        loads[4].wait()
        loads[5].wait()
    with jax.named_scope("rows_rest"):
        gather_step(0, 2)
        gather_step(1, 1)
        gather_step(0, 3)
        gather_step(1, 2)
        gather_step(0, 4)
    with jax.named_scope("activate_first"):
        activate(0)
    with jax.named_scope("rows_last"):
        gather_step(1, 3)
        gather_step(1, 4)
    with jax.named_scope("hidden_first"):
        lower(h, 0, True)
        hidden_step(0, 1)
    with jax.named_scope("activate_second"):
        activate(1)
    with jax.named_scope("hidden_rest"):
        hidden_step(0, 2)
        mixing = mix()
        lower(h, 1, True)
        hidden_step(1, 1)
        hidden_step(0, 3)
        hidden_step(1, 2)
        hidden_step(0, 4)
        hand_over(0)
        hidden_step(1, 3)
        hidden_step(1, 4)
        hand_over(1)

    with jax.named_scope("collect"):
        expert_rows = jnp.concatenate([collect(m) for m in range(micro)], axis=0)
        back_send[...] = dot(sorted_rows[...], expert_rows).reshape(n, slots, width)

    def back(to, at):
        return pltpu.make_async_remote_copy(
            src_ref=back_send.at[to],
            dst_ref=back_recv.at[at],
            send_sem=back_sem.at[0, to],
            recv_sem=back_sem.at[1, at],
            device_id={"head": jnp.int32(to), "exp": h},
            device_id_type=MESH,
        )

    with jax.named_scope("return"):
        for j in range(n):

            @pl.when(jnp.logical_or(h != e, h != j))
            def _():
                back(j, e).start()

            @pl.when(jnp.logical_and(h == e, h == j))
            def _():
                back_recv[j] = back_send[j]

        for j in range(n):

            @pl.when(jnp.logical_or(h != e, e != j))
            def _():
                back(j, j).wait_recv()

    returned = back_recv[...].reshape(places, width)
    returned = returned.astype(BF16)
    result = stream_all[e].astype(F32)
    for piece in pieces(mixing):
        result += dot(piece, returned)
    out_ref[...] = result.reshape(micro, group, width).astype(BF16)

    swaps = [swap_att, swap_aux, swap_part, swap_stream, *swaps_down]
    for pair in first_swaps:
        swaps += pair
    for swap in swaps:
        swap.wait_send()
    for ring in rings_a + rings_b + rings_h:
        ring.wait_send()
    for j in range(n):

        @pl.when(jnp.logical_or(h != e, h != j))
        def _():
            back(j, e).wait_send()


def per_device(
    n,
    query,
    cache_keys,
    cache_values,
    lengths,
    out_proj,
    residual,
    norm_gain,
    router,
    expert_ids,
    gate_weight,
    up_weight,
    down_weight,
):
    micro, group, width = query.shape
    tokens, slots = micro * group, micro * SLOTS
    features = n * width
    hidden_width = gate_weight.shape[2]
    vmem = pl.BlockSpec(memory_space=pltpu.VMEM)
    smem = pl.BlockSpec(memory_space=pltpu.SMEM)
    anywhere = pl.BlockSpec(memory_space=pl.ANY)

    block_rows = n * SLOTS
    all_rows = n * block_rows
    scratch = [
        pltpu.VMEM(cache_keys.shape, BF16),
        pltpu.VMEM(cache_values.shape, BF16),
        pltpu.VMEM(out_proj.shape, BF16),
        pltpu.VMEM((features, 2 * hidden_width), BF16),
        pltpu.VMEM(down_weight.shape[1:], BF16),
        pltpu.VMEM((n, 2 * n, width), BF16),
        pltpu.VMEM((n, tokens, width), BF16),
        pltpu.VMEM((n, tokens, width), F32),
        pltpu.VMEM((n, tokens, width), BF16),
        pltpu.VMEM((n, tokens, width), BF16),
        pltpu.VMEM((n, tokens, width), BF16),
        pltpu.VMEM((micro, n, n // 2 * SLOTS, width), BF16),
        pltpu.VMEM((micro, n, n // 2 * SLOTS, width), BF16),
        pltpu.VMEM((n, micro, block_rows, features // 2), BF16),
        pltpu.VMEM((n, micro, block_rows, features // 2), BF16),
        pltpu.VMEM((micro, n // 2 * SLOTS, n // 2 * tokens), BF16),
        pltpu.VMEM((n * n // 2 * SLOTS, n * n // 2 * SLOTS), BF16),
        pltpu.VMEM((all_rows, all_rows), BF16),
        pltpu.VMEM((micro * block_rows, micro * block_rows), BF16),
        pltpu.VMEM((n, micro, all_rows, hidden_width), BF16),
        pltpu.VMEM((micro, n, block_rows, width), F32),
        pltpu.VMEM((micro, n, block_rows, width), BF16),
        pltpu.VMEM((micro, n, block_rows, width), BF16),
        pltpu.VMEM((n, slots, width), F32),
        pltpu.VMEM((n, slots, width), F32),
        pltpu.SemaphoreType.DMA((6,)),
        pltpu.SemaphoreType.DMA((10, 2, n - 1)),
        pltpu.SemaphoreType.DMA((3 * micro, 4, n // 2)),
        pltpu.SemaphoreType.DMA((2, n)),
    ]
    return pl.pallas_call(
        functools.partial(layer, n),
        out_shape=jax.ShapeDtypeStruct((micro, group, width), BF16),
        in_specs=[
            vmem,
            anywhere,
            anywhere,
            smem,
            anywhere,
            vmem,
            vmem,
            vmem,
            vmem,
            anywhere,
            anywhere,
            anywhere,
        ],
        out_specs=vmem,
        scratch_shapes=scratch,
        compiler_params=pltpu.CompilerParams(
            collective_id=0, has_side_effects=True, vmem_limit_bytes=60 * 1024 * 1024
        ),
    )(
        query,
        cache_keys,
        cache_values,
        lengths,
        out_proj,
        residual,
        norm_gain,
        router.T,
        expert_ids.transpose(0, 2, 1),
        gate_weight,
        up_weight,
        down_weight,
    )


def solution(mesh):
    in_specs = (
        P(None, ("req", "exp"), "head"),
        P(None, ("req", "exp"), None, "head"),
        P(None, ("req", "exp"), None, "head"),
        P(None, ("req", "exp")),
        P("head", "exp"),
        P(None, ("req", "head"), "exp"),
        P("exp"),
        P("exp", None),
        P(None, ("req", "head"), None),
        P("exp", None, ("req", "head")),
        P("exp", None, ("req", "head")),
        P("exp", "req", "head"),
    )
    out_specs = P(None, ("req", "head"), "exp")
    return jax.shard_map(
        functools.partial(per_device, mesh.shape["exp"]),
        mesh=mesh,
        in_specs=in_specs,
        out_specs=out_specs,
        check_vma=False,
    )
```

```python
import functools

import jax
import jax.numpy as jnp
from jax import lax
from jax.experimental import pallas as pl
from jax.experimental.pallas import tpu as pltpu
from jax.sharding import PartitionSpec as P

MESH = pl.DeviceIdType.MESH
HEAD_DIM = 128
SLOTS = 4
F32 = jnp.float32
BF16 = jnp.bfloat16


def iota(shape, axis):
    return lax.broadcasted_iota(jnp.int32, shape, axis)


def dot(a, b, **kw):
    return jnp.dot(a, b, preferred_element_type=F32, **kw)


def dot_t(a, b, **kw):
    return lax.dot_general(a, b, (((1,), (1,)), ((), ())), preferred_element_type=F32, **kw)


def pieces(x):
    high = x.astype(BF16)
    rest = x - high.astype(F32)
    middle = rest.astype(BF16)
    return high, middle, (rest - middle.astype(F32)).astype(BF16)


class Swap:
    def __init__(self, axis, me, n, src, dst, sems):
        self.axis, self.me, self.n, self.src, self.dst, self.sems = axis, me, n, src, dst, sems

    def copy(self, src, dst, to):
        return pltpu.make_async_remote_copy(
            src_ref=src,
            dst_ref=dst,
            send_sem=self.sems.at[0],
            recv_sem=self.sems.at[1],
            device_id={self.axis: to},
            device_id_type=MESH,
        )

    def start(self):
        for d in sorted(range(1, self.n), key=lambda d: -min(d, self.n - d)):
            to = lax.rem(self.me + d, self.n)
            self.copy(self.src(to), self.dst.at[self.me], to).start()

    def everything(self):
        others = self.dst.at[pl.ds(0, self.n - 1)]
        return self.copy(others, others, lax.rem(self.me + 1, self.n))

    def wait_recv(self):
        self.everything().wait_recv()

    def wait_send(self):
        self.everything().wait_send()


class Ring:
    def __init__(self, axis, me, n, block_ref, sems):
        self.axis, self.me, self.n, self.block_ref, self.sems = axis, me, n, block_ref, sems
        self.half = n // 2

    def block(self, way, k):
        return lax.rem(self.me + (self.n - k if way == 0 else k), self.n)

    def copy(self, way, k, block):
        ref = self.block_ref(block)
        if k == self.half:
            rows = ref.shape[0] // 2
            ref = ref.at[pl.ds(way * rows, rows)]
        to = lax.rem(self.me + (1 if way == 0 else self.n - 1), self.n)
        return pltpu.make_async_remote_copy(
            src_ref=ref,
            dst_ref=ref,
            send_sem=self.sems.at[2 * way, k - 1],
            recv_sem=self.sems.at[2 * way + 1, k - 1],
            device_id={self.axis: to},
            device_id_type=MESH,
        )

    def send(self, way, k):
        self.copy(way, k, self.block(way, k - 1)).start()

    def start(self):
        for way in (0, 1):
            self.send(way, 1)

    def step(self, k):
        for way in (0, 1):
            self.copy(way, k, self.block(way, k)).wait_recv()
            if k < self.half:
                self.send(way, k + 1)

    def blocks(self, k):
        return [self.block(way, k) for way in ((0, 1) if k < self.half else (0,))]

    def wait_send(self):
        for k in range(1, self.half + 1):
            for way in (0, 1):
                self.copy(way, k, self.block(way, k - 1)).wait_send()


def layer(
    n,
    query_ref,
    keys_hbm,
    values_hbm,
    lengths_ref,
    proj_hbm,
    residual_ref,
    gain_ref,
    router_ref,
    ids_ref,
    gate_hbm,
    up_hbm,
    down_hbm,
    out_ref,
    keys,
    values,
    proj,
    wide,
    down,
    aux_all,
    att_all,
    part_own,
    part_send,
    part_recv,
    stream_all,
    first_a,
    first_b,
    rows_a,
    rows_b,
    take_all,
    ordered,
    crossed,
    sorted_rows,
    hidden,
    acc,
    down_send,
    down_recv,
    back_send,
    back_recv,
    load_sem,
    swap_sem,
    ring_sem,
    back_sem,
):
    micro, group, width = query_ref.shape
    tokens = micro * group
    slots = micro * SLOTS
    r, h, e = lax.axis_index("req"), lax.axis_index("head"), lax.axis_index("exp")
    features = n * width
    hidden_width = gate_hbm.shape[2]
    positions = keys_hbm.shape[2]

    barrier = pltpu.get_barrier_semaphore()
    for axis, me in (("exp", e), ("head", h), ("req", r)):
        for d in range(1, n):
            pl.semaphore_signal(
                barrier, inc=1, device_id={axis: lax.rem(me + d, n)}, device_id_type=MESH
            )
    for j in range(n):

        @pl.when(jnp.logical_or(h != e, e != j))
        def _():
            pl.semaphore_signal(
                barrier, inc=1, device_id={"head": e, "exp": jnp.int32(j)}, device_id_type=MESH
            )

    loads = [
        pltpu.make_async_copy(keys_hbm, keys, load_sem.at[0]),
        pltpu.make_async_copy(values_hbm, values, load_sem.at[1]),
        pltpu.make_async_copy(proj_hbm, proj, load_sem.at[2]),
        pltpu.make_async_copy(gate_hbm.at[0], wide.at[:, pl.ds(0, hidden_width)], load_sem.at[3]),
        pltpu.make_async_copy(
            up_hbm.at[0], wide.at[:, pl.ds(hidden_width, hidden_width)], load_sem.at[4]
        ),
        pltpu.make_async_copy(down_hbm.at[0], down, load_sem.at[5]),
    ]
    for load in loads:
        load.start()

    with jax.named_scope("attention"):
        per_key = width // HEAD_DIM
        queries = query_ref[...].astype(F32).reshape(tokens, width)
        queries = jnp.concatenate(
            [queries[:, j * HEAD_DIM : (j + 1) * HEAD_DIM] for j in range(per_key)], axis=0
        ).astype(BF16)
        columns = tokens * positions
        owner = iota((1, columns), 1) // positions
        limit = jnp.zeros((1, columns), jnp.int32)
        for t in range(tokens):
            limit = jnp.where(owner == t, lengths_ref[t // group, t % group], limit)
        valid = lax.rem(iota((1, columns), 1), positions) < limit
        owner = jnp.where(valid, owner, -1)
        allowed = lax.rem(iota((per_key * tokens, columns), 0), tokens) == owner
        loads[0].wait()
        scores = dot_t(queries, keys[...].reshape(columns, HEAD_DIM)) * HEAD_DIM ** (-0.5)
        scores = jnp.where(allowed, scores, F32(-1e30))
        exponents = jnp.exp(scores - jnp.max(scores, axis=-1, keepdims=True))
        weights = (exponents / jnp.sum(exponents, axis=-1, keepdims=True)).astype(BF16)
        loads[1].wait()
        mixed = dot(weights, values[...].reshape(columns, HEAD_DIM))
        for j in range(per_key):
            att_all[e, :, j * HEAD_DIM : (j + 1) * HEAD_DIM] = mixed[
                j * tokens : (j + 1) * tokens
            ].astype(BF16)
        gain = jnp.broadcast_to(gain_ref[...].astype(F32).reshape(1, width), (n, width))
        aux_all[e] = jnp.concatenate([router_ref[...].astype(F32), gain], axis=0).astype(BF16)

    with jax.named_scope("entry"):
        pl.semaphore_wait(barrier, 3 * (n - 1) + n - jnp.where(h == e, 1, 0))

    swap_att = Swap("exp", e, n, lambda to: att_all.at[e], att_all, swap_sem.at[0])
    swap_aux = Swap("exp", e, n, lambda to: aux_all.at[e], aux_all, swap_sem.at[1])
    swap_att.start()
    swap_aux.start()

    with jax.named_scope("routing"):
        places = n * slots
        diagonal = iota((group, group), 0) == iota((group, group), 1)

        def upright(row):
            return jnp.sum(jnp.where(diagonal, row, F32(0.0)), axis=-1, keepdims=True)

        ids = [
            jnp.concatenate(
                [upright(ids_ref[m][k : k + 1, :].astype(F32)) for m in range(micro)], axis=0
            ).astype(jnp.int32)
            for k in range(2)
        ]
        token_at = iota((tokens, places), 0)
        column = iota((tokens, places), 1)
        hots = [(ids[k] == column // slots).astype(F32) for k in range(2)]
        earlier_of = (
            (iota((tokens, tokens), 1) < iota((tokens, tokens), 0))
            & (iota((tokens, tokens), 1) // group == iota((tokens, tokens), 0) // group)
        ).astype(BF16)
        earlier = dot(earlier_of, (hots[0] + hots[1]).astype(BF16))
        fits = (lax.rem(column, SLOTS).astype(F32) == earlier) & (
            lax.rem(column, slots) // SLOTS == token_at // group
        )
        chosen_at = [jnp.where(fits, hot, F32(0.0)) for hot in hots]
        sel_own = dot_t(
            ((iota((slots, places), 1) - slots * e) == iota((slots, places), 0)).astype(BF16),
            (chosen_at[0] + chosen_at[1]).astype(BF16),
        ).astype(BF16)

        chunks = n // 2
        packed = chunks * SLOTS
        block_rows = n * SLOTS
        all_rows = n * block_rows
        for m in range(micro):
            pick = (
                iota((packed, slots), 1) == m * SLOTS + lax.rem(iota((packed, slots), 0), SLOTS)
            ).astype(BF16)
            spread = (
                lax.rem(iota((tokens, chunks * tokens), 1), tokens)
                == iota((tokens, chunks * tokens), 0)
            ).astype(BF16)
            same = (
                iota((packed, chunks * tokens), 0) // SLOTS
                == iota((packed, chunks * tokens), 1) // tokens
            )
            take = dot(dot(pick, sel_own).astype(BF16), spread)
            take_all[m] = jnp.where(same, take, F32(0.0)).astype(BF16)

        def one_hot(size, place):
            return (place(iota((size, size), 0)) == iota((size, size), 1)).astype(BF16)

        ordered[...] = one_hot(
            n * packed,
            lambda i: lax.rem(i, block_rows) // SLOTS * packed
            + i // block_rows * SLOTS
            + lax.rem(i, SLOTS),
        )
        crossed[...] = one_hot(
            all_rows,
            lambda i: lax.rem(i, block_rows) // SLOTS * block_rows
            + i // block_rows * SLOTS
            + lax.rem(i, SLOTS),
        )
        sorted_rows[...] = one_hot(
            micro * block_rows,
            lambda i: lax.rem(i, slots) // SLOTS * block_rows + i // slots * SLOTS + lax.rem(i, SLOTS),
        )

    with jax.named_scope("projection"):
        loads[2].wait()
        swap_att.wait_recv()
        partial = dot(att_all[...].reshape(n * tokens, width), proj[...]).reshape(n, tokens, width)
        part_own[...] = partial
        part_send[...] = partial.astype(BF16)
        swap_part = Swap(
            "head", h, n, lambda to: part_send.at[to], part_recv, swap_sem.at[2]
        )
        swap_part.start()
    with jax.named_scope("stream"):
        projected = part_own[h]
        residual = residual_ref[...].astype(F32).reshape(tokens, width)
        swap_part.wait_recv()
        for d in range(1, n):
            projected += part_recv[lax.rem(h + d, n)].astype(F32)
        stream_all[e] = (residual + projected).astype(BF16)
        swap_stream = Swap(
            "exp", e, n, lambda to: stream_all.at[e], stream_all, swap_sem.at[3]
        )
        swap_stream.start()
    with jax.named_scope("norm"):
        swap_aux.wait_recv()
        swap_stream.wait_recv()

        squares = jnp.zeros((tokens, width), F32)
        for j in range(n):
            block = stream_all[j].astype(F32)
            squares += block * block
        inverse = lax.rsqrt(jnp.sum(squares, axis=-1, keepdims=True) / features + 1e-05)
        normed = []
        for j in range(n):
            full = stream_all[j].astype(F32) * aux_all[j].astype(F32)[n : n + 1] * inverse
            normed.append(full)
        stacked = [
            jnp.concatenate([full.astype(BF16) for full in normed[i * chunks : (i + 1) * chunks]], axis=0)
            for i in range(2)
        ]
        first_swaps = []
        for m in range(micro):
            take = take_all[m]
            first_a[m, h] = dot(take, stacked[0]).astype(BF16)
            first_b[m, r] = dot(take, stacked[1]).astype(BF16)
            swap_a = Swap(
                "head",
                h,
                n,
                lambda to, m=m: first_a.at[m, h],
                first_a.at[m],
                swap_sem.at[4 + 2 * m],
            )
            swap_b = Swap(
                "req",
                r,
                n,
                lambda to, m=m: first_b.at[m, r],
                first_b.at[m],
                swap_sem.at[5 + 2 * m],
            )
            swap_a.start()
            swap_b.start()
            first_swaps.append((swap_a, swap_b))

    half = features // 2

    def settle(first, rows_to):
        y = dot(ordered[...], first[...].reshape(n * packed, width)).astype(BF16)
        for c in range(chunks):
            rows_to[:, pl.ds(c * width, width)] = y[c * block_rows : (c + 1) * block_rows]

    rings_a = [
        Ring("req", r, n, lambda b, m=m: rows_a.at[b, m], ring_sem.at[m]) for m in range(micro)
    ]
    rings_b = [
        Ring("head", h, n, lambda b, m=m: rows_b.at[b, m], ring_sem.at[micro + m])
        for m in range(micro)
    ]
    rings_h = [
        Ring("head", h, n, lambda b, m=m: hidden.at[b, m], ring_sem.at[2 * micro + m])
        for m in range(micro)
    ]

    def settle_a(m):
        first_swaps[m][0].wait_recv()
        settle(first_a.at[m], rows_a.at[r, m])

    def settle_b(m):
        first_swaps[m][1].wait_recv()
        settle(first_b.at[m], rows_b.at[h, m])

    with jax.named_scope("settle"):
        settle_a(0)
        rings_a[0].start()
        settle_b(0)
        rings_b[0].start()
        settle_a(1)
        settle_b(1)

    def mix():
        logits = jnp.zeros((tokens, 2 * n), F32)
        for j in range(n):
            full = stream_all[j].astype(F32) * aux_all[j].astype(F32)[n : n + 1] * inverse
            for piece in pieces(full):
                logits += dot_t(piece, aux_all[j])
        lane = iota((tokens, 2 * n), 1)
        powers = [
            jnp.exp(jnp.sum(jnp.where(lane == ids[k], logits, F32(0.0)), axis=-1, keepdims=True))
            for k in range(2)
        ]
        total = powers[0] + powers[1]
        return powers[0] / total * chosen_at[0] + powers[1] / total * chosen_at[1]

    def activate(m):
        x = rows_a[:, m].reshape(all_rows, half)
        y = dot(x, wide[pl.ds(0, half), :])
        x = dot(crossed[...], rows_b[:, m].reshape(all_rows, half)).astype(BF16)
        y += dot(x, wide[pl.ds(half, half), :])
        gated, upward = y[:, :hidden_width], y[:, hidden_width:]
        hidden[h, m] = (gated / (1.0 + jnp.exp(-gated)) * upward).astype(BF16)
        rings_h[m].start()

    def lower(b, m, first=False):
        y = dot(
            hidden[b, m], down[pl.ds(pl.multiple_of(b * hidden_width, hidden_width), hidden_width), :]
        ).reshape(n, block_rows, width)
        acc[m] = y if first else acc[m] + y

    def gather_step(m, k):
        rings_a[m].step(k)
        rings_b[m].step(k)

    def hidden_step(m, k):
        rings_h[m].step(k)
        for b in rings_h[m].blocks(k):
            lower(b, m)

    swaps_down = [
        Swap(
            "req",
            r,
            n,
            lambda to, m=m: down_send.at[m, to],
            down_recv.at[m],
            swap_sem.at[8 + m],
        )
        for m in range(micro)
    ]

    def hand_over(m):
        down_send[m] = acc[m].astype(BF16)
        swaps_down[m].start()

    def collect(m):
        total = acc[m, r]
        swaps_down[m].wait_recv()
        for d in range(1, n):
            total += down_recv[m, lax.rem(r + d, n)].astype(F32)
        return total.astype(BF16)

    with jax.named_scope("rows_first"):
        gather_step(0, 1)
        rings_a[1].start()
        rings_b[1].start()
        for load in loads[3:]:
            load.wait()
        for swap in (swap_att, swap_aux, swap_part, swap_stream):
            swap.wait_send()
    with jax.named_scope("rows_rest"):
        gather_step(0, 2)
        gather_step(1, 1)
        gather_step(0, 3)
        gather_step(1, 2)
        gather_step(0, 4)
        activate(0)
        gather_step(1, 3)
        lower(h, 0, True)
        for pair in first_swaps:
            for swap in pair:
                swap.wait_send()
        gather_step(1, 4)
    with jax.named_scope("hidden_units"):
        hidden_step(0, 1)
        activate(1)
        hidden_step(0, 2)
        lower(h, 1, True)
        hidden_step(1, 1)
        mixing = mix()
        hidden_step(0, 3)
        hidden_step(1, 2)
        for ring in rings_a + rings_b:
            ring.wait_send()
        hidden_step(0, 4)
        hand_over(0)
        hidden_step(1, 3)
        hidden_step(1, 4)
        hand_over(1)
        for ring in rings_h:
            ring.wait_send()

    with jax.named_scope("collect"):
        expert_rows = jnp.concatenate([collect(m) for m in range(micro)], axis=0)
        back_send[...] = dot(sorted_rows[...], expert_rows).reshape(n, slots, width)

    def back(to, at):
        return pltpu.make_async_remote_copy(
            src_ref=back_send.at[to],
            dst_ref=back_recv.at[at],
            send_sem=back_sem.at[0],
            recv_sem=back_sem.at[1],
            device_id={"head": jnp.int32(to), "exp": h},
            device_id_type=MESH,
        )

    with jax.named_scope("return"):
        for j in range(n):

            @pl.when(jnp.logical_or(h != e, h != j))
            def _():
                back(j, e).start()

            @pl.when(jnp.logical_and(h == e, h == j))
            def _():
                back_recv[j] = back_send[j]

        for swap in swaps_down:
            swap.wait_send()
        for count, here in ((n, h != e), (n - 1, h == e)):

            @pl.when(here)
            def _():
                those = back_recv.at[pl.ds(0, count)]
                every = pltpu.make_async_remote_copy(
                    src_ref=those,
                    dst_ref=those,
                    send_sem=back_sem.at[0],
                    recv_sem=back_sem.at[1],
                    device_id={"exp": lax.rem(e + 1, n)},
                    device_id_type=MESH,
                )
                every.wait_recv()
                every.wait_send()

    returned = back_recv[...].reshape(places, width)
    returned = returned.astype(BF16)
    result = stream_all[e].astype(F32)
    for piece in pieces(mixing):
        result += dot(piece, returned)
    out_ref[...] = result.reshape(micro, group, width).astype(BF16)


def per_device(
    n,
    query,
    cache_keys,
    cache_values,
    lengths,
    out_proj,
    residual,
    norm_gain,
    router,
    expert_ids,
    gate_weight,
    up_weight,
    down_weight,
):
    micro, group, width = query.shape
    tokens, slots = micro * group, micro * SLOTS
    features = n * width
    hidden_width = gate_weight.shape[2]
    vmem = pl.BlockSpec(memory_space=pltpu.VMEM)
    smem = pl.BlockSpec(memory_space=pltpu.SMEM)
    anywhere = pl.BlockSpec(memory_space=pl.ANY)

    block_rows = n * SLOTS
    all_rows = n * block_rows
    scratch = [
        pltpu.VMEM(cache_keys.shape, BF16),
        pltpu.VMEM(cache_values.shape, BF16),
        pltpu.VMEM(out_proj.shape, BF16),
        pltpu.VMEM((features, 2 * hidden_width), BF16),
        pltpu.VMEM(down_weight.shape[1:], BF16),
        pltpu.VMEM((n, 2 * n, width), BF16),
        pltpu.VMEM((n, tokens, width), BF16),
        pltpu.VMEM((n, tokens, width), F32),
        pltpu.VMEM((n, tokens, width), BF16),
        pltpu.VMEM((n, tokens, width), BF16),
        pltpu.VMEM((n, tokens, width), BF16),
        pltpu.VMEM((micro, n, n // 2 * SLOTS, width), BF16),
        pltpu.VMEM((micro, n, n // 2 * SLOTS, width), BF16),
        pltpu.VMEM((n, micro, block_rows, features // 2), BF16),
        pltpu.VMEM((n, micro, block_rows, features // 2), BF16),
        pltpu.VMEM((micro, n // 2 * SLOTS, n // 2 * tokens), BF16),
        pltpu.VMEM((n * n // 2 * SLOTS, n * n // 2 * SLOTS), BF16),
        pltpu.VMEM((all_rows, all_rows), BF16),
        pltpu.VMEM((micro * block_rows, micro * block_rows), BF16),
        pltpu.VMEM((n, micro, all_rows, hidden_width), BF16),
        pltpu.VMEM((micro, n, block_rows, width), F32),
        pltpu.VMEM((micro, n, block_rows, width), BF16),
        pltpu.VMEM((micro, n, block_rows, width), BF16),
        pltpu.VMEM((n, slots, width), F32),
        pltpu.VMEM((n, slots, width), F32),
        pltpu.SemaphoreType.DMA((6,)),
        pltpu.SemaphoreType.DMA((10, 2)),
        pltpu.SemaphoreType.DMA((3 * micro, 4, n // 2)),
        pltpu.SemaphoreType.DMA((2,)),
    ]
    return pl.pallas_call(
        functools.partial(layer, n),
        out_shape=jax.ShapeDtypeStruct((micro, group, width), BF16),
        in_specs=[
            vmem,
            anywhere,
            anywhere,
            smem,
            anywhere,
            vmem,
            vmem,
            vmem,
            vmem,
            anywhere,
            anywhere,
            anywhere,
        ],
        out_specs=vmem,
        scratch_shapes=scratch,
        compiler_params=pltpu.CompilerParams(
            collective_id=0, has_side_effects=True, vmem_limit_bytes=60 * 1024 * 1024
        ),
    )(
        query,
        cache_keys,
        cache_values,
        lengths,
        out_proj,
        residual,
        norm_gain,
        router.T,
        expert_ids.transpose(0, 2, 1),
        gate_weight,
        up_weight,
        down_weight,
    )


def solution(mesh):
    in_specs = (
        P(None, ("req", "exp"), "head"),
        P(None, ("req", "exp"), None, "head"),
        P(None, ("req", "exp"), None, "head"),
        P(None, ("req", "exp")),
        P("head", "exp"),
        P(None, ("req", "head"), "exp"),
        P("exp"),
        P("exp", None),
        P(None, ("req", "head"), None),
        P("exp", None, ("req", "head")),
        P("exp", None, ("req", "head")),
        P("exp", "req", "head"),
    )
    out_specs = P(None, ("req", "head"), "exp")
    return jax.shard_map(
        functools.partial(per_device, mesh.shape["exp"]),
        mesh=mesh,
        in_specs=in_specs,
        out_specs=out_specs,
        check_vma=False,
    )
```

```python
import functools

import jax
import jax.numpy as jnp
from jax import lax
from jax.experimental import pallas as pl
from jax.experimental.pallas import tpu as pltpu
from jax.sharding import PartitionSpec as P

MESH = pl.DeviceIdType.MESH
HEAD_DIM = 128
SLOTS = 4
F32 = jnp.float32
BF16 = jnp.bfloat16


def iota(shape, axis):
    return lax.broadcasted_iota(jnp.int32, shape, axis)


def dot(a, b, **kw):
    return jnp.dot(a, b, preferred_element_type=F32, **kw)


def dot_t(a, b, **kw):
    return lax.dot_general(a, b, (((1,), (1,)), ((), ())), preferred_element_type=F32, **kw)


def pieces(x):
    high = x.astype(BF16)
    rest = x - high.astype(F32)
    middle = rest.astype(BF16)
    return high, middle, (rest - middle.astype(F32)).astype(BF16)


class Swap:
    def __init__(self, axis, me, n, src, dst, sems):
        self.axis, self.me, self.n, self.src, self.dst, self.sems = axis, me, n, src, dst, sems

    def copy(self, src, dst, to):
        return pltpu.make_async_remote_copy(
            src_ref=src,
            dst_ref=dst,
            send_sem=self.sems.at[0],
            recv_sem=self.sems.at[1],
            device_id={self.axis: to},
            device_id_type=MESH,
        )

    def start(self):
        for d in sorted(range(1, self.n), key=lambda d: -min(d, self.n - d)):
            to = lax.rem(self.me + d, self.n)
            self.copy(self.src(to), self.dst.at[self.me], to).start()

    def everything(self):
        others = self.dst.at[pl.ds(0, self.n - 1)]
        return self.copy(others, others, lax.rem(self.me + 1, self.n))

    def wait_recv(self):
        self.everything().wait_recv()

    def wait_send(self):
        self.everything().wait_send()


class Ring:
    def __init__(self, axis, me, n, block_ref, sems):
        self.axis, self.me, self.n, self.block_ref, self.sems = axis, me, n, block_ref, sems
        self.half = n // 2

    def block(self, way, k):
        return lax.rem(self.me + (self.n - k if way == 0 else k), self.n)

    def copy(self, way, k, block):
        ref = self.block_ref(block)
        if k == self.half:
            rows = ref.shape[0] // 2
            ref = ref.at[pl.ds(way * rows, rows)]
        to = lax.rem(self.me + (1 if way == 0 else self.n - 1), self.n)
        return pltpu.make_async_remote_copy(
            src_ref=ref,
            dst_ref=ref,
            send_sem=self.sems.at[2 * way, k - 1],
            recv_sem=self.sems.at[2 * way + 1, k - 1],
            device_id={self.axis: to},
            device_id_type=MESH,
        )

    def send(self, way, k):
        self.copy(way, k, self.block(way, k - 1)).start()

    def start(self):
        for way in (0, 1):
            self.send(way, 1)

    def step(self, k):
        for way in (0, 1):
            self.copy(way, k, self.block(way, k)).wait_recv()
            if k < self.half:
                self.send(way, k + 1)

    def blocks(self, k):
        return [self.block(way, k) for way in ((0, 1) if k < self.half else (0,))]

    def wait_send(self):
        for k in range(1, self.half + 1):
            for way in (0, 1):
                self.copy(way, k, self.block(way, k - 1)).wait_send()


def layer(
    n,
    query_ref,
    keys_hbm,
    values_hbm,
    lengths_ref,
    proj_hbm,
    residual_ref,
    gain_ref,
    router_ref,
    ids_ref,
    gate_hbm,
    up_hbm,
    down_hbm,
    out_ref,
    keys,
    values,
    proj,
    wide,
    down,
    aux_all,
    att_all,
    part_own,
    part_send,
    part_recv,
    stream_all,
    first_a,
    first_b,
    first_w,
    rows_a,
    rows_b,
    rows_w,
    take_half,
    take_whole,
    ordered,
    crossed,
    sorted_rows,
    hidden,
    acc,
    down_send,
    down_recv,
    back_send,
    back_recv,
    load_sem,
    swap_sem,
    ring_sem,
    back_sem,
):
    micro, group, width = query_ref.shape
    tokens = micro * group
    slots = micro * SLOTS
    r, h, e = lax.axis_index("req"), lax.axis_index("head"), lax.axis_index("exp")
    features = n * width
    hidden_width = gate_hbm.shape[2]
    positions = keys_hbm.shape[2]

    barrier = pltpu.get_barrier_semaphore()
    for axis, me in (("exp", e), ("head", h), ("req", r)):
        for d in range(1, n):
            pl.semaphore_signal(
                barrier, inc=1, device_id={axis: lax.rem(me + d, n)}, device_id_type=MESH
            )
    for j in range(n):

        @pl.when(jnp.logical_or(h != e, e != j))
        def _():
            pl.semaphore_signal(
                barrier, inc=1, device_id={"head": e, "exp": jnp.int32(j)}, device_id_type=MESH
            )

    loads = [
        pltpu.make_async_copy(keys_hbm, keys, load_sem.at[0]),
        pltpu.make_async_copy(values_hbm, values, load_sem.at[1]),
        pltpu.make_async_copy(proj_hbm, proj, load_sem.at[2]),
        pltpu.make_async_copy(gate_hbm.at[0], wide.at[:, pl.ds(0, hidden_width)], load_sem.at[3]),
        pltpu.make_async_copy(
            up_hbm.at[0], wide.at[:, pl.ds(hidden_width, hidden_width)], load_sem.at[4]
        ),
        pltpu.make_async_copy(down_hbm.at[0], down, load_sem.at[5]),
    ]
    for load in loads:
        load.start()

    with jax.named_scope("attention"):
        per_key = width // HEAD_DIM
        queries = query_ref[...].astype(F32).reshape(tokens, width)
        queries = jnp.concatenate(
            [queries[:, j * HEAD_DIM : (j + 1) * HEAD_DIM] for j in range(per_key)], axis=0
        ).astype(BF16)
        columns = tokens * positions
        owner = iota((1, columns), 1) // positions
        limit = jnp.zeros((1, columns), jnp.int32)
        for t in range(tokens):
            limit = jnp.where(owner == t, lengths_ref[t // group, t % group], limit)
        valid = lax.rem(iota((1, columns), 1), positions) < limit
        owner = jnp.where(valid, owner, -1)
        allowed = lax.rem(iota((per_key * tokens, columns), 0), tokens) == owner
        loads[0].wait()
        scores = dot_t(queries, keys[...].reshape(columns, HEAD_DIM)) * HEAD_DIM ** (-0.5)
        scores = jnp.where(allowed, scores, F32(-1e30))
        exponents = jnp.exp(scores - jnp.max(scores, axis=-1, keepdims=True))
        weights = (exponents / jnp.sum(exponents, axis=-1, keepdims=True)).astype(BF16)
        loads[1].wait()
        mixed = dot(weights, values[...].reshape(columns, HEAD_DIM))
        for j in range(per_key):
            att_all[e, :, j * HEAD_DIM : (j + 1) * HEAD_DIM] = mixed[
                j * tokens : (j + 1) * tokens
            ].astype(BF16)
        gain = jnp.broadcast_to(gain_ref[...].astype(F32).reshape(1, width), (n, width))
        aux_all[e] = jnp.concatenate([router_ref[...].astype(F32), gain], axis=0).astype(BF16)

    with jax.named_scope("entry"):
        pl.semaphore_wait(barrier, 3 * (n - 1) + n - jnp.where(h == e, 1, 0))

    swap_att = Swap("exp", e, n, lambda to: att_all.at[e], att_all, swap_sem.at[0])
    swap_aux = Swap("exp", e, n, lambda to: aux_all.at[e], aux_all, swap_sem.at[1])
    swap_att.start()
    swap_aux.start()

    with jax.named_scope("routing"):
        places = n * slots
        diagonal = iota((group, group), 0) == iota((group, group), 1)

        def upright(row):
            return jnp.sum(jnp.where(diagonal, row, F32(0.0)), axis=-1, keepdims=True)

        ids = [
            jnp.concatenate(
                [upright(ids_ref[m][k : k + 1, :].astype(F32)) for m in range(micro)], axis=0
            ).astype(jnp.int32)
            for k in range(2)
        ]
        token_at = iota((tokens, places), 0)
        column = iota((tokens, places), 1)
        hots = [(ids[k] == column // slots).astype(F32) for k in range(2)]
        earlier_of = (
            (iota((tokens, tokens), 1) < iota((tokens, tokens), 0))
            & (iota((tokens, tokens), 1) // group == iota((tokens, tokens), 0) // group)
        ).astype(BF16)
        earlier = dot(earlier_of, (hots[0] + hots[1]).astype(BF16))
        fits = (lax.rem(column, SLOTS).astype(F32) == earlier) & (
            lax.rem(column, slots) // SLOTS == token_at // group
        )
        chosen_at = [jnp.where(fits, hot, F32(0.0)) for hot in hots]
        sel_own = dot_t(
            ((iota((slots, places), 1) - slots * e) == iota((slots, places), 0)).astype(BF16),
            (chosen_at[0] + chosen_at[1]).astype(BF16),
        ).astype(BF16)

        chunks = n // 2
        packed = chunks * SLOTS
        block_rows = n * SLOTS
        all_rows = n * block_rows
        def taking(m, parts):
            shape = (parts * SLOTS, parts * tokens)
            pick = (
                iota((shape[0], slots), 1) == m * SLOTS + lax.rem(iota((shape[0], slots), 0), SLOTS)
            ).astype(BF16)
            spread = (
                lax.rem(iota((tokens, shape[1]), 1), tokens) == iota((tokens, shape[1]), 0)
            ).astype(BF16)
            same = iota(shape, 0) // SLOTS == iota(shape, 1) // tokens
            table = dot(dot(pick, sel_own).astype(BF16), spread)
            return jnp.where(same, table, F32(0.0)).astype(BF16)

        take_half[...] = taking(0, chunks)
        take_whole[...] = taking(1, n)

        def one_hot(size, place):
            return (place(iota((size, size), 0)) == iota((size, size), 1)).astype(BF16)

        ordered[...] = one_hot(
            n * packed,
            lambda i: lax.rem(i, block_rows) // SLOTS * packed
            + i // block_rows * SLOTS
            + lax.rem(i, SLOTS),
        )
        crossed[...] = one_hot(
            all_rows,
            lambda i: lax.rem(i, block_rows) // SLOTS * block_rows
            + i // block_rows * SLOTS
            + lax.rem(i, SLOTS),
        )
        sorted_rows[...] = one_hot(
            micro * block_rows,
            lambda i: lax.rem(i, slots) // SLOTS * block_rows + i // slots * SLOTS + lax.rem(i, SLOTS),
        )

    with jax.named_scope("projection"):
        loads[2].wait()
        swap_att.wait_recv()
        partial = dot(att_all[...].reshape(n * tokens, width), proj[...]).reshape(n, tokens, width)
        part_own[...] = partial
        part_send[...] = partial.astype(BF16)
        swap_part = Swap(
            "head", h, n, lambda to: part_send.at[to], part_recv, swap_sem.at[2]
        )
        swap_part.start()
    with jax.named_scope("stream"):
        projected = part_own[h]
        residual = residual_ref[...].astype(F32).reshape(tokens, width)
        swap_part.wait_recv()
        for d in range(1, n):
            projected += part_recv[lax.rem(h + d, n)].astype(F32)
        stream_all[e] = (residual + projected).astype(BF16)
        swap_stream = Swap(
            "exp", e, n, lambda to: stream_all.at[e], stream_all, swap_sem.at[3]
        )
        swap_stream.start()
    with jax.named_scope("norm"):
        swap_aux.wait_recv()
        swap_stream.wait_recv()

        squares = jnp.zeros((tokens, width), F32)
        for j in range(n):
            block = stream_all[j].astype(F32)
            squares += block * block
        inverse = lax.rsqrt(jnp.sum(squares, axis=-1, keepdims=True) / features + 1e-05)
        normed = []
        for j in range(n):
            full = stream_all[j].astype(F32) * aux_all[j].astype(F32)[n : n + 1] * inverse
            normed.append(full)
        stacked = [
            jnp.concatenate([full.astype(BF16) for full in normed[i * chunks : (i + 1) * chunks]], axis=0)
            for i in range(2)
        ]
        first_a[h] = dot(take_half[...], stacked[0]).astype(BF16)
        first_b[r] = dot(take_half[...], stacked[1]).astype(BF16)
        swap_a = Swap("head", h, n, lambda to: first_a.at[h], first_a, swap_sem.at[4])
        swap_b = Swap("req", r, n, lambda to: first_b.at[r], first_b, swap_sem.at[5])
        swap_w = Swap("head", h, n, lambda to: first_w.at[h], first_w, swap_sem.at[6])
        swap_a.start()
        swap_b.start()
        first_w[h] = dot(take_whole[...], jnp.concatenate(stacked, axis=0)).astype(BF16)
        swap_w.start()

    half = features // 2

    def settle(swap, order, first, rows_to):
        swap.wait_recv()
        y = dot(order[...], first[...].reshape(n * first.shape[1], width)).astype(BF16)
        for c in range(first.shape[1] // SLOTS):
            rows_to[:, pl.ds(c * width, width)] = y[c * block_rows : (c + 1) * block_rows]

    ring_a = Ring("req", r, n, lambda b: rows_a.at[b], ring_sem.at[0])
    ring_b = Ring("head", h, n, lambda b: rows_b.at[b], ring_sem.at[1])
    ring_w = Ring("req", r, n, lambda b: rows_w.at[b], ring_sem.at[2])
    rings_h = [
        Ring("head", h, n, lambda b, m=m: hidden.at[b, m], ring_sem.at[3 + m])
        for m in range(micro)
    ]

    with jax.named_scope("settle"):
        settle(swap_a, ordered, first_a, rows_a.at[r])
        ring_a.start()
        settle(swap_b, ordered, first_b, rows_b.at[h])
        ring_b.start()
        settle(swap_w, crossed, first_w, rows_w.at[r])

    def mix():
        logits = jnp.zeros((tokens, 2 * n), F32)
        for j in range(n):
            full = stream_all[j].astype(F32) * aux_all[j].astype(F32)[n : n + 1] * inverse
            for piece in pieces(full):
                logits += dot_t(piece, aux_all[j])
        lane = iota((tokens, 2 * n), 1)
        powers = [
            jnp.exp(jnp.sum(jnp.where(lane == ids[k], logits, F32(0.0)), axis=-1, keepdims=True))
            for k in range(2)
        ]
        total = powers[0] + powers[1]
        return powers[0] / total * chosen_at[0] + powers[1] / total * chosen_at[1]

    def activate(m):
        if m == 0:
            y = dot(rows_a[...].reshape(all_rows, half), wide[pl.ds(0, half), :])
            x = dot(crossed[...], rows_b[...].reshape(all_rows, half)).astype(BF16)
            y += dot(x, wide[pl.ds(half, half), :])
        else:
            y = dot(rows_w[...].reshape(all_rows, features), wide[...])
        gated, upward = y[:, :hidden_width], y[:, hidden_width:]
        hidden[h, m] = (gated / (1.0 + jnp.exp(-gated)) * upward).astype(BF16)
        rings_h[m].start()

    def lower(b, m, first=False):
        y = dot(
            hidden[b, m], down[pl.ds(pl.multiple_of(b * hidden_width, hidden_width), hidden_width), :]
        ).reshape(n, block_rows, width)
        acc[m] = y if first else acc[m] + y

    def gather_step(k):
        ring_a.step(k)
        ring_b.step(k)

    def hidden_step(m, k):
        rings_h[m].step(k)
        for b in rings_h[m].blocks(k):
            lower(b, m)

    swaps_down = [
        Swap(
            "req",
            r,
            n,
            lambda to, m=m: down_send.at[m, to],
            down_recv.at[m],
            swap_sem.at[7 + m],
        )
        for m in range(micro)
    ]

    def hand_over(m):
        down_send[m] = acc[m].astype(BF16)
        swaps_down[m].start()

    def collect(m):
        total = acc[m, r]
        swaps_down[m].wait_recv()
        for d in range(1, n):
            total += down_recv[m, lax.rem(r + d, n)].astype(F32)
        return total.astype(BF16)

    with jax.named_scope("rows"):
        gather_step(1)
        ring_w.start()
        for load in loads[3:]:
            load.wait()
        for swap in (swap_att, swap_aux, swap_part, swap_stream):
            swap.wait_send()
        gather_step(2)
        ring_w.step(1)
        gather_step(3)
        ring_w.step(2)
        gather_step(4)
        activate(0)
        lower(h, 0, True)
        ring_w.step(3)
    with jax.named_scope("hidden_units"):
        hidden_step(0, 1)
        for swap in (swap_a, swap_b, swap_w):
            swap.wait_send()
        ring_w.step(4)
        activate(1)
        hidden_step(0, 2)
        lower(h, 1, True)
        mixing = mix()
        hidden_step(0, 3)
        hidden_step(1, 1)
        hidden_step(0, 4)
        hand_over(0)
        for ring in (ring_a, ring_b, ring_w):
            ring.wait_send()
        hidden_step(1, 2)
        hidden_step(1, 3)
        first_rows = collect(0)
        hidden_step(1, 4)
        hand_over(1)
        for ring in rings_h:
            ring.wait_send()

    with jax.named_scope("collect"):
        expert_rows = jnp.concatenate([first_rows, collect(1)], axis=0)
        back_send[...] = dot(sorted_rows[...], expert_rows).reshape(n, slots, width)

    def back(to, at):
        return pltpu.make_async_remote_copy(
            src_ref=back_send.at[to],
            dst_ref=back_recv.at[at],
            send_sem=back_sem.at[0],
            recv_sem=back_sem.at[1],
            device_id={"head": jnp.int32(to), "exp": h},
            device_id_type=MESH,
        )

    with jax.named_scope("return"):
        for j in range(n):

            @pl.when(jnp.logical_or(h != e, h != j))
            def _():
                back(j, e).start()

            @pl.when(jnp.logical_and(h == e, h == j))
            def _():
                back_recv[j] = back_send[j]

        for swap in swaps_down:
            swap.wait_send()
        for count, here in ((n, h != e), (n - 1, h == e)):

            @pl.when(here)
            def _():
                those = back_recv.at[pl.ds(0, count)]
                every = pltpu.make_async_remote_copy(
                    src_ref=those,
                    dst_ref=those,
                    send_sem=back_sem.at[0],
                    recv_sem=back_sem.at[1],
                    device_id={"exp": lax.rem(e + 1, n)},
                    device_id_type=MESH,
                )
                every.wait_recv()
                every.wait_send()

    returned = back_recv[...].reshape(places, width)
    returned = returned.astype(BF16)
    result = stream_all[e].astype(F32)
    for piece in pieces(mixing):
        result += dot(piece, returned)
    out_ref[...] = result.reshape(micro, group, width).astype(BF16)


def per_device(
    n,
    query,
    cache_keys,
    cache_values,
    lengths,
    out_proj,
    residual,
    norm_gain,
    router,
    expert_ids,
    gate_weight,
    up_weight,
    down_weight,
):
    micro, group, width = query.shape
    tokens, slots = micro * group, micro * SLOTS
    features = n * width
    hidden_width = gate_weight.shape[2]
    vmem = pl.BlockSpec(memory_space=pltpu.VMEM)
    smem = pl.BlockSpec(memory_space=pltpu.SMEM)
    anywhere = pl.BlockSpec(memory_space=pl.ANY)

    block_rows = n * SLOTS
    all_rows = n * block_rows
    scratch = [
        pltpu.VMEM(cache_keys.shape, BF16),
        pltpu.VMEM(cache_values.shape, BF16),
        pltpu.VMEM(out_proj.shape, BF16),
        pltpu.VMEM((features, 2 * hidden_width), BF16),
        pltpu.VMEM(down_weight.shape[1:], BF16),
        pltpu.VMEM((n, 2 * n, width), BF16),
        pltpu.VMEM((n, tokens, width), BF16),
        pltpu.VMEM((n, tokens, width), F32),
        pltpu.VMEM((n, tokens, width), BF16),
        pltpu.VMEM((n, tokens, width), BF16),
        pltpu.VMEM((n, tokens, width), BF16),
        pltpu.VMEM((n, n // 2 * SLOTS, width), BF16),
        pltpu.VMEM((n, n // 2 * SLOTS, width), BF16),
        pltpu.VMEM((n, n * SLOTS, width), BF16),
        pltpu.VMEM((n, block_rows, features // 2), BF16),
        pltpu.VMEM((n, block_rows, features // 2), BF16),
        pltpu.VMEM((n, block_rows, features), BF16),
        pltpu.VMEM((n // 2 * SLOTS, n // 2 * tokens), BF16),
        pltpu.VMEM((n * SLOTS, n * tokens), BF16),
        pltpu.VMEM((n * n // 2 * SLOTS, n * n // 2 * SLOTS), BF16),
        pltpu.VMEM((all_rows, all_rows), BF16),
        pltpu.VMEM((micro * block_rows, micro * block_rows), BF16),
        pltpu.VMEM((n, micro, all_rows, hidden_width), BF16),
        pltpu.VMEM((micro, n, block_rows, width), F32),
        pltpu.VMEM((micro, n, block_rows, width), BF16),
        pltpu.VMEM((micro, n, block_rows, width), BF16),
        pltpu.VMEM((n, slots, width), F32),
        pltpu.VMEM((n, slots, width), F32),
        pltpu.SemaphoreType.DMA((6,)),
        pltpu.SemaphoreType.DMA((9, 2)),
        pltpu.SemaphoreType.DMA((3 + micro, 4, n // 2)),
        pltpu.SemaphoreType.DMA((2,)),
    ]
    return pl.pallas_call(
        functools.partial(layer, n),
        out_shape=jax.ShapeDtypeStruct((micro, group, width), BF16),
        in_specs=[
            vmem,
            anywhere,
            anywhere,
            smem,
            anywhere,
            vmem,
            vmem,
            vmem,
            vmem,
            anywhere,
            anywhere,
            anywhere,
        ],
        out_specs=vmem,
        scratch_shapes=scratch,
        compiler_params=pltpu.CompilerParams(
            collective_id=0, has_side_effects=True, vmem_limit_bytes=60 * 1024 * 1024
        ),
    )(
        query,
        cache_keys,
        cache_values,
        lengths,
        out_proj,
        residual,
        norm_gain,
        router.T,
        expert_ids.transpose(0, 2, 1),
        gate_weight,
        up_weight,
        down_weight,
    )


def solution(mesh):
    in_specs = (
        P(None, ("req", "exp"), "head"),
        P(None, ("req", "exp"), None, "head"),
        P(None, ("req", "exp"), None, "head"),
        P(None, ("req", "exp")),
        P("head", "exp"),
        P(None, ("req", "head"), "exp"),
        P("exp"),
        P("exp", None),
        P(None, ("req", "head"), None),
        P("exp", None, ("req", "head")),
        P("exp", None, ("req", "head")),
        P("exp", "req", "head"),
    )
    out_specs = P(None, ("req", "head"), "exp")
    return jax.shard_map(
        functools.partial(per_device, mesh.shape["exp"]),
        mesh=mesh,
        in_specs=in_specs,
        out_specs=out_specs,
        check_vma=False,
    )
```

```python
import functools

import jax
import jax.numpy as jnp
from jax import lax
from jax.experimental import pallas as pl
from jax.experimental.pallas import tpu as pltpu
from jax.sharding import PartitionSpec as P

MESH = pl.DeviceIdType.MESH
HEAD_DIM = 128
SLOTS = 4
F32 = jnp.float32
BF16 = jnp.bfloat16


def iota(shape, axis):
    return lax.broadcasted_iota(jnp.int32, shape, axis)


def dot(a, b, **kw):
    return jnp.dot(a, b, preferred_element_type=F32, **kw)


def dot_t(a, b, **kw):
    return lax.dot_general(a, b, (((1,), (1,)), ((), ())), preferred_element_type=F32, **kw)


def pieces(x):
    high = x.astype(BF16)
    rest = x - high.astype(F32)
    middle = rest.astype(BF16)
    return high, middle, (rest - middle.astype(F32)).astype(BF16)


class Swap:
    def __init__(self, axis, me, n, src, dst, sems):
        self.axis, self.me, self.n, self.src, self.dst, self.sems = axis, me, n, src, dst, sems

    def copy(self, src, dst, to):
        return pltpu.make_async_remote_copy(
            src_ref=src,
            dst_ref=dst,
            send_sem=self.sems.at[0],
            recv_sem=self.sems.at[1],
            device_id={self.axis: to},
            device_id_type=MESH,
        )

    def start(self):
        for d in sorted(range(1, self.n), key=lambda d: -min(d, self.n - d)):
            to = lax.rem(self.me + d, self.n)
            self.copy(self.src(to), self.dst.at[self.me], to).start()

    def everything(self):
        others = self.dst.at[pl.ds(0, self.n - 1)]
        return self.copy(others, others, lax.rem(self.me + 1, self.n))

    def wait_recv(self):
        self.everything().wait_recv()

    def wait_send(self):
        self.everything().wait_send()


class Ring:
    def __init__(self, axis, me, n, block_ref, sems):
        self.axis, self.me, self.n, self.block_ref, self.sems = axis, me, n, block_ref, sems
        self.half = n // 2

    def block(self, way, k):
        return lax.rem(self.me + (self.n - k if way == 0 else k), self.n)

    def copy(self, way, k, block):
        ref = self.block_ref(block)
        if k == self.half:
            rows = ref.shape[0] // 2
            ref = ref.at[pl.ds(way * rows, rows)]
        to = lax.rem(self.me + (1 if way == 0 else self.n - 1), self.n)
        return pltpu.make_async_remote_copy(
            src_ref=ref,
            dst_ref=ref,
            send_sem=self.sems.at[2 * way, k - 1],
            recv_sem=self.sems.at[2 * way + 1, k - 1],
            device_id={self.axis: to},
            device_id_type=MESH,
        )

    def send(self, way, k):
        self.copy(way, k, self.block(way, k - 1)).start()

    def start(self):
        for way in (0, 1):
            self.send(way, 1)

    def step(self, k):
        for way in (0, 1):
            self.copy(way, k, self.block(way, k)).wait_recv()
            if k < self.half:
                self.send(way, k + 1)

    def blocks(self, k):
        return [self.block(way, k) for way in ((0, 1) if k < self.half else (0,))]

    def wait_send(self):
        for k in range(1, self.half + 1):
            for way in (0, 1):
                self.copy(way, k, self.block(way, k - 1)).wait_send()


def layer(
    n,
    query_ref,
    keys_hbm,
    values_hbm,
    lengths_ref,
    proj_hbm,
    residual_ref,
    gain_ref,
    router_ref,
    ids_ref,
    gate_hbm,
    up_hbm,
    down_hbm,
    out_ref,
    keys,
    values,
    proj,
    wide,
    down,
    aux_all,
    att_all,
    part_own,
    part_send,
    part_recv,
    stream_all,
    first_a,
    first_b,
    rows_a,
    rows_b,
    take_all,
    ordered,
    crossed,
    sorted_rows,
    hidden,
    acc,
    down_send,
    down_recv,
    back_send,
    back_recv,
    load_sem,
    swap_sem,
    ring_sem,
    back_sem,
):
    micro, group, width = query_ref.shape
    tokens = micro * group
    slots = micro * SLOTS
    r, h, e = lax.axis_index("req"), lax.axis_index("head"), lax.axis_index("exp")
    features = n * width
    hidden_width = gate_hbm.shape[2]
    positions = keys_hbm.shape[2]

    barrier = pltpu.get_barrier_semaphore()
    for axis, me in (("exp", e), ("head", h), ("req", r)):
        for d in range(1, n):
            pl.semaphore_signal(
                barrier, inc=1, device_id={axis: lax.rem(me + d, n)}, device_id_type=MESH
            )
    for j in range(n):

        @pl.when(jnp.logical_or(h != e, e != j))
        def _():
            pl.semaphore_signal(
                barrier, inc=1, device_id={"head": e, "exp": jnp.int32(j)}, device_id_type=MESH
            )

    loads = [
        pltpu.make_async_copy(keys_hbm, keys, load_sem.at[0]),
        pltpu.make_async_copy(values_hbm, values, load_sem.at[1]),
        pltpu.make_async_copy(proj_hbm, proj, load_sem.at[2]),
        pltpu.make_async_copy(gate_hbm.at[0], wide.at[:, pl.ds(0, hidden_width)], load_sem.at[3]),
        pltpu.make_async_copy(
            up_hbm.at[0], wide.at[:, pl.ds(hidden_width, hidden_width)], load_sem.at[4]
        ),
        pltpu.make_async_copy(down_hbm.at[0], down, load_sem.at[5]),
    ]
    for load in loads:
        load.start()

    with jax.named_scope("attention"):
        per_key = width // HEAD_DIM
        queries = query_ref[...].astype(F32).reshape(tokens, width)
        queries = jnp.concatenate(
            [queries[:, j * HEAD_DIM : (j + 1) * HEAD_DIM] for j in range(per_key)], axis=0
        ).astype(BF16)
        columns = tokens * positions
        owner = iota((1, columns), 1) // positions
        limit = jnp.zeros((1, columns), jnp.int32)
        for t in range(tokens):
            limit = jnp.where(owner == t, lengths_ref[t // group, t % group], limit)
        valid = lax.rem(iota((1, columns), 1), positions) < limit
        owner = jnp.where(valid, owner, -1)
        allowed = lax.rem(iota((per_key * tokens, columns), 0), tokens) == owner
        loads[0].wait()
        scores = dot_t(queries, keys[...].reshape(columns, HEAD_DIM)) * HEAD_DIM ** (-0.5)
        scores = jnp.where(allowed, scores, F32(-1e30))
        exponents = jnp.exp(scores - jnp.max(scores, axis=-1, keepdims=True))
        weights = (exponents / jnp.sum(exponents, axis=-1, keepdims=True)).astype(BF16)
        loads[1].wait()
        mixed = dot(weights, values[...].reshape(columns, HEAD_DIM))
        for j in range(per_key):
            att_all[e, :, j * HEAD_DIM : (j + 1) * HEAD_DIM] = mixed[
                j * tokens : (j + 1) * tokens
            ].astype(BF16)
        gain = jnp.broadcast_to(gain_ref[...].astype(F32).reshape(1, width), (n, width))
        aux_all[e] = jnp.concatenate([router_ref[...].astype(F32), gain], axis=0).astype(BF16)

    with jax.named_scope("entry"):
        pl.semaphore_wait(barrier, 3 * (n - 1) + n - jnp.where(h == e, 1, 0))

    swap_att = Swap("exp", e, n, lambda to: att_all.at[e], att_all, swap_sem.at[0])
    swap_aux = Swap("exp", e, n, lambda to: aux_all.at[e], aux_all, swap_sem.at[1])
    swap_att.start()
    swap_aux.start()

    with jax.named_scope("routing"):
        places = n * slots
        diagonal = iota((group, group), 0) == iota((group, group), 1)

        def upright(row):
            return jnp.sum(jnp.where(diagonal, row, F32(0.0)), axis=-1, keepdims=True)

        ids = [
            jnp.concatenate(
                [upright(ids_ref[m][k : k + 1, :].astype(F32)) for m in range(micro)], axis=0
            ).astype(jnp.int32)
            for k in range(2)
        ]
        token_at = iota((tokens, places), 0)
        column = iota((tokens, places), 1)
        hots = [(ids[k] == column // slots).astype(F32) for k in range(2)]
        earlier_of = (
            (iota((tokens, tokens), 1) < iota((tokens, tokens), 0))
            & (iota((tokens, tokens), 1) // group == iota((tokens, tokens), 0) // group)
        ).astype(BF16)
        earlier = dot(earlier_of, (hots[0] + hots[1]).astype(BF16))
        fits = (lax.rem(column, SLOTS).astype(F32) == earlier) & (
            lax.rem(column, slots) // SLOTS == token_at // group
        )
        chosen_at = [jnp.where(fits, hot, F32(0.0)) for hot in hots]
        sel_own = dot_t(
            ((iota((slots, places), 1) - slots * e) == iota((slots, places), 0)).astype(BF16),
            (chosen_at[0] + chosen_at[1]).astype(BF16),
        ).astype(BF16)

        chunks = n // 2
        packed = chunks * SLOTS
        block_rows = n * SLOTS
        all_rows = n * block_rows
        for m in range(micro):
            pick = (
                iota((packed, slots), 1) == m * SLOTS + lax.rem(iota((packed, slots), 0), SLOTS)
            ).astype(BF16)
            spread = (
                lax.rem(iota((tokens, chunks * tokens), 1), tokens)
                == iota((tokens, chunks * tokens), 0)
            ).astype(BF16)
            same = (
                iota((packed, chunks * tokens), 0) // SLOTS
                == iota((packed, chunks * tokens), 1) // tokens
            )
            take = dot(dot(pick, sel_own).astype(BF16), spread)
            take_all[m] = jnp.where(same, take, F32(0.0)).astype(BF16)

        def one_hot(size, place):
            return (place(iota((size, size), 0)) == iota((size, size), 1)).astype(BF16)

        ordered[...] = one_hot(
            n * packed,
            lambda i: lax.rem(i, block_rows) // SLOTS * packed
            + i // block_rows * SLOTS
            + lax.rem(i, SLOTS),
        )
        crossed[...] = one_hot(
            all_rows,
            lambda i: lax.rem(i, block_rows) // SLOTS * block_rows
            + i // block_rows * SLOTS
            + lax.rem(i, SLOTS),
        )
        sorted_rows[...] = one_hot(
            micro * block_rows,
            lambda i: lax.rem(i, slots) // SLOTS * block_rows + i // slots * SLOTS + lax.rem(i, SLOTS),
        )

    with jax.named_scope("projection"):
        loads[2].wait()
        swap_att.wait_recv()
        partial = dot(att_all[...].reshape(n * tokens, width), proj[...]).reshape(n, tokens, width)
        part_own[...] = partial
        part_send[...] = partial.astype(BF16)
        swap_part = Swap(
            "head", h, n, lambda to: part_send.at[to], part_recv, swap_sem.at[2]
        )
        swap_part.start()
    with jax.named_scope("stream"):
        projected = part_own[h]
        residual = residual_ref[...].astype(F32).reshape(tokens, width)
        swap_part.wait_recv()
        for d in range(1, n):
            projected += part_recv[lax.rem(h + d, n)].astype(F32)
        stream_all[e] = (residual + projected).astype(BF16)
        swap_stream = Swap(
            "exp", e, n, lambda to: stream_all.at[e], stream_all, swap_sem.at[3]
        )
        swap_stream.start()
    with jax.named_scope("norm"):
        swap_aux.wait_recv()
        swap_stream.wait_recv()

        squares = jnp.zeros((tokens, width), F32)
        for j in range(n):
            block = stream_all[j].astype(F32)
            squares += block * block
        inverse = lax.rsqrt(jnp.sum(squares, axis=-1, keepdims=True) / features + 1e-05)
        normed = []
        for j in range(n):
            full = stream_all[j].astype(F32) * aux_all[j].astype(F32)[n : n + 1] * inverse
            normed.append(full)
        stacked = [
            jnp.concatenate([full.astype(BF16) for full in normed[i * chunks : (i + 1) * chunks]], axis=0)
            for i in range(2)
        ]
        first_swaps = []
        for m in range(micro):
            take = take_all[m]
            first_a[m, h] = dot(take, stacked[0]).astype(BF16)
            first_b[m, r] = dot(take, stacked[1]).astype(BF16)
            swap_a = Swap(
                "head",
                h,
                n,
                lambda to, m=m: first_a.at[m, h],
                first_a.at[m],
                swap_sem.at[4 + 2 * m],
            )
            swap_b = Swap(
                "req",
                r,
                n,
                lambda to, m=m: first_b.at[m, r],
                first_b.at[m],
                swap_sem.at[5 + 2 * m],
            )
            swap_a.start()
            swap_b.start()
            first_swaps.append((swap_a, swap_b))

    half = features // 2

    def settle(first, rows_to):
        y = dot(ordered[...], first[...].reshape(n * packed, width)).astype(BF16)
        for c in range(chunks):
            rows_to[:, pl.ds(c * width, width)] = y[c * block_rows : (c + 1) * block_rows]

    rings_a = [
        Ring("req", r, n, lambda b, m=m: rows_a.at[b, m], ring_sem.at[m]) for m in range(micro)
    ]
    rings_b = [
        Ring("head", h, n, lambda b, m=m: rows_b.at[b, m], ring_sem.at[micro + m])
        for m in range(micro)
    ]
    rings_h = [
        Ring("head", h, n, lambda b, m=m: hidden.at[b, m], ring_sem.at[2 * micro + m])
        for m in range(micro)
    ]

    def settle_a(m):
        first_swaps[m][0].wait_recv()
        settle(first_a.at[m], rows_a.at[r, m])

    def settle_b(m):
        first_swaps[m][1].wait_recv()
        settle(first_b.at[m], rows_b.at[h, m])

    with jax.named_scope("settle"):
        settle_a(0)
        rings_a[0].start()
        settle_b(0)
        rings_b[0].start()
        settle_a(1)
        settle_b(1)

    def mix():
        logits = jnp.zeros((tokens, 2 * n), F32)
        for j in range(n):
            full = stream_all[j].astype(F32) * aux_all[j].astype(F32)[n : n + 1] * inverse
            for piece in pieces(full):
                logits += dot_t(piece, aux_all[j])
        lane = iota((tokens, 2 * n), 1)
        powers = [
            jnp.exp(jnp.sum(jnp.where(lane == ids[k], logits, F32(0.0)), axis=-1, keepdims=True))
            for k in range(2)
        ]
        total = powers[0] + powers[1]
        return powers[0] / total * chosen_at[0] + powers[1] / total * chosen_at[1]

    def activate(m):
        x = rows_a[:, m].reshape(all_rows, half)
        y = dot(x, wide[pl.ds(0, half), :])
        x = dot(crossed[...], rows_b[:, m].reshape(all_rows, half)).astype(BF16)
        y += dot(x, wide[pl.ds(half, half), :])
        gated, upward = y[:, :hidden_width], y[:, hidden_width:]
        hidden[h, m] = (gated / (1.0 + jnp.exp(-gated)) * upward).astype(BF16)
        rings_h[m].start()

    def lower(b, m, first=False):
        y = dot(
            hidden[b, m], down[pl.ds(pl.multiple_of(b * hidden_width, hidden_width), hidden_width), :]
        ).reshape(n, block_rows, width)
        acc[m] = y if first else acc[m] + y

    def gather_step(m, k):
        rings_a[m].step(k)
        rings_b[m].step(k)

    def hidden_step(m, k, first=False):
        rings_h[m].step(k)
        if first:
            lower(h, m, True)
        for b in rings_h[m].blocks(k):
            lower(b, m)

    swaps_down = [
        Swap(
            "req",
            r,
            n,
            lambda to, m=m: down_send.at[m, to],
            down_recv.at[m],
            swap_sem.at[8 + m],
        )
        for m in range(micro)
    ]

    def hand_over(m):
        down_send[m] = acc[m].astype(BF16)
        swaps_down[m].start()

    def collect(m):
        total = acc[m, r]
        swaps_down[m].wait_recv()
        for d in range(1, n):
            total += down_recv[m, lax.rem(r + d, n)].astype(F32)
        return total.astype(BF16)

    with jax.named_scope("rows"):
        rings_a[1].start()
        rings_b[1].start()
        gather_step(0, 1)
        for load in loads[3:]:
            load.wait()
        gather_step(1, 1)
        for swap in (swap_att, swap_aux, swap_part, swap_stream):
            swap.wait_send()
        gather_step(0, 2)
        gather_step(1, 2)
        gather_step(0, 3)
        gather_step(1, 3)
        gather_step(0, 4)
        activate(0)
        gather_step(1, 4)
    with jax.named_scope("hidden_units"):
        activate(1)
        hidden_step(0, 1, True)
        hidden_step(1, 1, True)
        for pair in first_swaps:
            for swap in pair:
                swap.wait_send()
        hidden_step(0, 2)
        mixing = mix()
        hidden_step(1, 2)
        for ring in rings_a + rings_b:
            ring.wait_send()
        hidden_step(0, 3)
        hidden_step(1, 3)
        hidden_step(0, 4)
        hand_over(0)
        hidden_step(1, 4)
        hand_over(1)
        for ring in rings_h:
            ring.wait_send()

    with jax.named_scope("collect"):
        expert_rows = jnp.concatenate([collect(m) for m in range(micro)], axis=0)
        back_send[...] = dot(sorted_rows[...], expert_rows).reshape(n, slots, width)

    def back(to, at):
        return pltpu.make_async_remote_copy(
            src_ref=back_send.at[to],
            dst_ref=back_recv.at[at],
            send_sem=back_sem.at[0],
            recv_sem=back_sem.at[1],
            device_id={"head": jnp.int32(to), "exp": h},
            device_id_type=MESH,
        )

    with jax.named_scope("return"):
        for j in range(n):

            @pl.when(jnp.logical_or(h != e, h != j))
            def _():
                back(j, e).start()

            @pl.when(jnp.logical_and(h == e, h == j))
            def _():
                back_recv[j] = back_send[j]

        for swap in swaps_down:
            swap.wait_send()
        for count, here in ((n, h != e), (n - 1, h == e)):

            @pl.when(here)
            def _():
                those = back_recv.at[pl.ds(0, count)]
                every = pltpu.make_async_remote_copy(
                    src_ref=those,
                    dst_ref=those,
                    send_sem=back_sem.at[0],
                    recv_sem=back_sem.at[1],
                    device_id={"exp": lax.rem(e + 1, n)},
                    device_id_type=MESH,
                )
                every.wait_recv()
                every.wait_send()

    returned = back_recv[...].reshape(places, width)
    returned = returned.astype(BF16)
    result = stream_all[e].astype(F32)
    for piece in pieces(mixing):
        result += dot(piece, returned)
    out_ref[...] = result.reshape(micro, group, width).astype(BF16)


def per_device(
    n,
    query,
    cache_keys,
    cache_values,
    lengths,
    out_proj,
    residual,
    norm_gain,
    router,
    expert_ids,
    gate_weight,
    up_weight,
    down_weight,
):
    micro, group, width = query.shape
    tokens, slots = micro * group, micro * SLOTS
    features = n * width
    hidden_width = gate_weight.shape[2]
    vmem = pl.BlockSpec(memory_space=pltpu.VMEM)
    smem = pl.BlockSpec(memory_space=pltpu.SMEM)
    anywhere = pl.BlockSpec(memory_space=pl.ANY)

    block_rows = n * SLOTS
    all_rows = n * block_rows
    scratch = [
        pltpu.VMEM(cache_keys.shape, BF16),
        pltpu.VMEM(cache_values.shape, BF16),
        pltpu.VMEM(out_proj.shape, BF16),
        pltpu.VMEM((features, 2 * hidden_width), BF16),
        pltpu.VMEM(down_weight.shape[1:], BF16),
        pltpu.VMEM((n, 2 * n, width), BF16),
        pltpu.VMEM((n, tokens, width), BF16),
        pltpu.VMEM((n, tokens, width), F32),
        pltpu.VMEM((n, tokens, width), BF16),
        pltpu.VMEM((n, tokens, width), BF16),
        pltpu.VMEM((n, tokens, width), BF16),
        pltpu.VMEM((micro, n, n // 2 * SLOTS, width), BF16),
        pltpu.VMEM((micro, n, n // 2 * SLOTS, width), BF16),
        pltpu.VMEM((n, micro, block_rows, features // 2), BF16),
        pltpu.VMEM((n, micro, block_rows, features // 2), BF16),
        pltpu.VMEM((micro, n // 2 * SLOTS, n // 2 * tokens), BF16),
        pltpu.VMEM((n * n // 2 * SLOTS, n * n // 2 * SLOTS), BF16),
        pltpu.VMEM((all_rows, all_rows), BF16),
        pltpu.VMEM((micro * block_rows, micro * block_rows), BF16),
        pltpu.VMEM((n, micro, all_rows, hidden_width), BF16),
        pltpu.VMEM((micro, n, block_rows, width), F32),
        pltpu.VMEM((micro, n, block_rows, width), BF16),
        pltpu.VMEM((micro, n, block_rows, width), BF16),
        pltpu.VMEM((n, slots, width), F32),
        pltpu.VMEM((n, slots, width), F32),
        pltpu.SemaphoreType.DMA((6,)),
        pltpu.SemaphoreType.DMA((10, 2)),
        pltpu.SemaphoreType.DMA((3 * micro, 4, n // 2)),
        pltpu.SemaphoreType.DMA((2,)),
    ]
    return pl.pallas_call(
        functools.partial(layer, n),
        out_shape=jax.ShapeDtypeStruct((micro, group, width), BF16),
        in_specs=[
            vmem,
            anywhere,
            anywhere,
            smem,
            anywhere,
            vmem,
            vmem,
            vmem,
            vmem,
            anywhere,
            anywhere,
            anywhere,
        ],
        out_specs=vmem,
        scratch_shapes=scratch,
        compiler_params=pltpu.CompilerParams(
            collective_id=0, has_side_effects=True, vmem_limit_bytes=60 * 1024 * 1024
        ),
    )(
        query,
        cache_keys,
        cache_values,
        lengths,
        out_proj,
        residual,
        norm_gain,
        router.T,
        expert_ids.transpose(0, 2, 1),
        gate_weight,
        up_weight,
        down_weight,
    )


def solution(mesh):
    in_specs = (
        P(None, ("req", "exp"), "head"),
        P(None, ("req", "exp"), None, "head"),
        P(None, ("req", "exp"), None, "head"),
        P(None, ("req", "exp")),
        P("head", "exp"),
        P(None, ("req", "head"), "exp"),
        P("exp"),
        P("exp", None),
        P(None, ("req", "head"), None),
        P("exp", None, ("req", "head")),
        P("exp", None, ("req", "head")),
        P("exp", "req", "head"),
    )
    out_specs = P(None, ("req", "head"), "exp")
    return jax.shard_map(
        functools.partial(per_device, mesh.shape["exp"]),
        mesh=mesh,
        in_specs=in_specs,
        out_specs=out_specs,
        check_vma=False,
    )
```

```python
import functools

import jax
import jax.numpy as jnp
from jax import lax
from jax.experimental import pallas as pl
from jax.experimental.pallas import tpu as pltpu
from jax.sharding import PartitionSpec as P

MESH = pl.DeviceIdType.MESH
HEAD_DIM = 128
SLOTS = 4
F32 = jnp.float32
BF16 = jnp.bfloat16


def iota(shape, axis):
    return lax.broadcasted_iota(jnp.int32, shape, axis)


def dot(a, b, **kw):
    return jnp.dot(a, b, preferred_element_type=F32, **kw)


def dot_t(a, b, **kw):
    return lax.dot_general(a, b, (((1,), (1,)), ((), ())), preferred_element_type=F32, **kw)


def pieces(x):
    high = x.astype(BF16)
    rest = x - high.astype(F32)
    middle = rest.astype(BF16)
    return high, middle, (rest - middle.astype(F32)).astype(BF16)


class Swap:
    def __init__(self, axis, me, n, src, dst, sems):
        self.axis, self.me, self.n, self.src, self.dst, self.sems = axis, me, n, src, dst, sems

    def copy(self, src, dst, to):
        return pltpu.make_async_remote_copy(
            src_ref=src,
            dst_ref=dst,
            send_sem=self.sems.at[0],
            recv_sem=self.sems.at[1],
            device_id={self.axis: to},
            device_id_type=MESH,
        )

    def start(self):
        for d in sorted(range(1, self.n), key=lambda d: -min(d, self.n - d)):
            to = lax.rem(self.me + d, self.n)
            self.copy(self.src(to), self.dst.at[self.me], to).start()

    def everything(self):
        others = self.dst.at[pl.ds(0, self.n - 1)]
        return self.copy(others, others, lax.rem(self.me + 1, self.n))

    def wait_recv(self):
        self.everything().wait_recv()

    def wait_send(self):
        self.everything().wait_send()


class Ring:
    def __init__(self, axis, me, n, block_ref, sems):
        self.axis, self.me, self.n, self.block_ref, self.sems = axis, me, n, block_ref, sems
        self.half = n // 2

    def block(self, way, k):
        return lax.rem(self.me + (self.n - k if way == 0 else k), self.n)

    def copy(self, way, k, block):
        ref = self.block_ref(block)
        if k == self.half:
            rows = ref.shape[0] // 2
            ref = ref.at[pl.ds(way * rows, rows)]
        to = lax.rem(self.me + (1 if way == 0 else self.n - 1), self.n)
        return pltpu.make_async_remote_copy(
            src_ref=ref,
            dst_ref=ref,
            send_sem=self.sems.at[2 * way, k - 1],
            recv_sem=self.sems.at[2 * way + 1, k - 1],
            device_id={self.axis: to},
            device_id_type=MESH,
        )

    def send(self, way, k):
        self.copy(way, k, self.block(way, k - 1)).start()

    def start(self):
        for way in (0, 1):
            self.send(way, 1)

    def step(self, k):
        for way in (0, 1):
            self.copy(way, k, self.block(way, k)).wait_recv()
            if k < self.half:
                self.send(way, k + 1)

    def blocks(self, k):
        return [self.block(way, k) for way in ((0, 1) if k < self.half else (0,))]

    def wait_send(self):
        for k in range(1, self.half + 1):
            for way in (0, 1):
                self.copy(way, k, self.block(way, k - 1)).wait_send()


def layer(
    n,
    query_ref,
    keys_hbm,
    values_hbm,
    lengths_ref,
    proj_hbm,
    residual_ref,
    gain_ref,
    router_ref,
    ids_ref,
    gate_hbm,
    up_hbm,
    down_hbm,
    out_ref,
    keys,
    values,
    proj,
    wide,
    down,
    aux_all,
    att_all,
    part_own,
    part_send,
    part_recv,
    stream_all,
    first_a,
    first_b,
    rows_a,
    rows_b,
    take_all,
    ordered,
    crossed,
    sorted_rows,
    hidden,
    acc,
    down_send,
    down_recv,
    back_send,
    back_recv,
    load_sem,
    swap_sem,
    ring_sem,
    back_sem,
):
    micro, group, width = query_ref.shape
    tokens = micro * group
    slots = micro * SLOTS
    r, h, e = lax.axis_index("req"), lax.axis_index("head"), lax.axis_index("exp")
    features = n * width
    hidden_width = gate_hbm.shape[2]
    positions = keys_hbm.shape[2]

    barrier = pltpu.get_barrier_semaphore()
    for axis, me in (("exp", e), ("head", h), ("req", r)):
        for d in range(1, n):
            pl.semaphore_signal(
                barrier, inc=1, device_id={axis: lax.rem(me + d, n)}, device_id_type=MESH
            )
    for j in range(n):

        @pl.when(jnp.logical_or(h != e, e != j))
        def _():
            pl.semaphore_signal(
                barrier, inc=1, device_id={"head": e, "exp": jnp.int32(j)}, device_id_type=MESH
            )

    loads = [
        pltpu.make_async_copy(keys_hbm, keys, load_sem.at[0]),
        pltpu.make_async_copy(values_hbm, values, load_sem.at[1]),
        pltpu.make_async_copy(proj_hbm, proj, load_sem.at[2]),
        pltpu.make_async_copy(gate_hbm.at[0], wide.at[:, pl.ds(0, hidden_width)], load_sem.at[3]),
        pltpu.make_async_copy(
            up_hbm.at[0], wide.at[:, pl.ds(hidden_width, hidden_width)], load_sem.at[4]
        ),
        pltpu.make_async_copy(down_hbm.at[0], down, load_sem.at[5]),
    ]
    for load in loads:
        load.start()

    with jax.named_scope("attention"):
        per_key = width // HEAD_DIM
        queries = query_ref[...].astype(F32).reshape(tokens, width)
        queries = jnp.concatenate(
            [queries[:, j * HEAD_DIM : (j + 1) * HEAD_DIM] for j in range(per_key)], axis=0
        ).astype(BF16)
        columns = tokens * positions
        owner = iota((1, columns), 1) // positions
        limit = jnp.zeros((1, columns), jnp.int32)
        for t in range(tokens):
            limit = jnp.where(owner == t, lengths_ref[t // group, t % group], limit)
        valid = lax.rem(iota((1, columns), 1), positions) < limit
        owner = jnp.where(valid, owner, -1)
        allowed = lax.rem(iota((per_key * tokens, columns), 0), tokens) == owner
        loads[0].wait()
        scores = dot_t(queries, keys[...].reshape(columns, HEAD_DIM)) * HEAD_DIM ** (-0.5)
        scores = jnp.where(allowed, scores, F32(-1e30))
        exponents = jnp.exp(scores - jnp.max(scores, axis=-1, keepdims=True))
        weights = (exponents / jnp.sum(exponents, axis=-1, keepdims=True)).astype(BF16)
        loads[1].wait()
        mixed = dot(weights, values[...].reshape(columns, HEAD_DIM))
        for j in range(per_key):
            att_all[e, :, j * HEAD_DIM : (j + 1) * HEAD_DIM] = mixed[
                j * tokens : (j + 1) * tokens
            ].astype(BF16)
        gain = jnp.broadcast_to(gain_ref[...].astype(F32).reshape(1, width), (n, width))
        aux_all[e] = jnp.concatenate([router_ref[...].astype(F32), gain], axis=0).astype(BF16)

    with jax.named_scope("entry"):
        pl.semaphore_wait(barrier, 3 * (n - 1) + n - jnp.where(h == e, 1, 0))

    swap_att = Swap("exp", e, n, lambda to: att_all.at[e], att_all, swap_sem.at[0])
    swap_aux = Swap("exp", e, n, lambda to: aux_all.at[e], aux_all, swap_sem.at[1])
    swap_att.start()
    swap_aux.start()

    with jax.named_scope("routing"):
        places = n * slots
        diagonal = iota((group, group), 0) == iota((group, group), 1)

        def upright(row):
            return jnp.sum(jnp.where(diagonal, row, F32(0.0)), axis=-1, keepdims=True)

        ids = [
            jnp.concatenate(
                [upright(ids_ref[m][k : k + 1, :].astype(F32)) for m in range(micro)], axis=0
            ).astype(jnp.int32)
            for k in range(2)
        ]
        token_at = iota((tokens, places), 0)
        column = iota((tokens, places), 1)
        hots = [(ids[k] == column // slots).astype(F32) for k in range(2)]
        earlier_of = (
            (iota((tokens, tokens), 1) < iota((tokens, tokens), 0))
            & (iota((tokens, tokens), 1) // group == iota((tokens, tokens), 0) // group)
        ).astype(BF16)
        earlier = dot(earlier_of, (hots[0] + hots[1]).astype(BF16))
        fits = (lax.rem(column, SLOTS).astype(F32) == earlier) & (
            lax.rem(column, slots) // SLOTS == token_at // group
        )
        chosen_at = [jnp.where(fits, hot, F32(0.0)) for hot in hots]
        sel_own = dot_t(
            ((iota((slots, places), 1) - slots * e) == iota((slots, places), 0)).astype(BF16),
            (chosen_at[0] + chosen_at[1]).astype(BF16),
        ).astype(BF16)

        chunks = n // 2
        packed = chunks * SLOTS
        block_rows = n * SLOTS
        all_rows = n * block_rows
        for m in range(micro):
            pick = (
                iota((packed, slots), 1) == m * SLOTS + lax.rem(iota((packed, slots), 0), SLOTS)
            ).astype(BF16)
            spread = (
                lax.rem(iota((tokens, chunks * tokens), 1), tokens)
                == iota((tokens, chunks * tokens), 0)
            ).astype(BF16)
            same = (
                iota((packed, chunks * tokens), 0) // SLOTS
                == iota((packed, chunks * tokens), 1) // tokens
            )
            take = dot(dot(pick, sel_own).astype(BF16), spread)
            take_all[m] = jnp.where(same, take, F32(0.0)).astype(BF16)

        def one_hot(size, place):
            return (place(iota((size, size), 0)) == iota((size, size), 1)).astype(BF16)

        ordered[...] = one_hot(
            n * packed,
            lambda i: lax.rem(i, block_rows) // SLOTS * packed
            + i // block_rows * SLOTS
            + lax.rem(i, SLOTS),
        )
        crossed[...] = one_hot(
            all_rows,
            lambda i: lax.rem(i, block_rows) // SLOTS * block_rows
            + i // block_rows * SLOTS
            + lax.rem(i, SLOTS),
        )
        sorted_rows[...] = one_hot(
            micro * block_rows,
            lambda i: lax.rem(i, slots) // SLOTS * block_rows + i // slots * SLOTS + lax.rem(i, SLOTS),
        )

    with jax.named_scope("projection"):
        loads[2].wait()
        swap_att.wait_recv()
        partial = dot(att_all[...].reshape(n * tokens, width), proj[...]).reshape(n, tokens, width)
        part_own[...] = partial
        part_send[...] = partial.astype(BF16)
        swap_part = Swap(
            "head", h, n, lambda to: part_send.at[to], part_recv, swap_sem.at[2]
        )
        swap_part.start()
    with jax.named_scope("stream"):
        projected = part_own[h]
        residual = residual_ref[...].astype(F32).reshape(tokens, width)
        swap_part.wait_recv()
        for d in range(1, n):
            projected += part_recv[lax.rem(h + d, n)].astype(F32)
        stream_all[e] = (residual + projected).astype(BF16)
        swap_stream = Swap(
            "exp", e, n, lambda to: stream_all.at[e], stream_all, swap_sem.at[3]
        )
        swap_stream.start()
    with jax.named_scope("norm"):
        swap_aux.wait_recv()
        swap_stream.wait_recv()

        squares = jnp.zeros((tokens, width), F32)
        for j in range(n):
            block = stream_all[j].astype(F32)
            squares += block * block
        inverse = lax.rsqrt(jnp.sum(squares, axis=-1, keepdims=True) / features + 1e-05)
        normed = []
        for j in range(n):
            full = stream_all[j].astype(F32) * aux_all[j].astype(F32)[n : n + 1] * inverse
            normed.append(full)
        stacked = [
            jnp.concatenate([full.astype(BF16) for full in normed[i * chunks : (i + 1) * chunks]], axis=0)
            for i in range(2)
        ]
        first_swaps = []
        for m in range(micro):
            take = take_all[m]
            first_a[m, h] = dot(take, stacked[0]).astype(BF16)
            first_b[m, r] = dot(take, stacked[1]).astype(BF16)
            swap_a = Swap(
                "head",
                h,
                n,
                lambda to, m=m: first_a.at[m, h],
                first_a.at[m],
                swap_sem.at[4 + 2 * m],
            )
            swap_b = Swap(
                "req",
                r,
                n,
                lambda to, m=m: first_b.at[m, r],
                first_b.at[m],
                swap_sem.at[5 + 2 * m],
            )
            swap_a.start()
            swap_b.start()
            first_swaps.append((swap_a, swap_b))

    half = features // 2

    def settle(first, rows_to):
        y = dot(ordered[...], first[...].reshape(n * packed, width)).astype(BF16)
        for c in range(chunks):
            rows_to[:, pl.ds(c * width, width)] = y[c * block_rows : (c + 1) * block_rows]

    rings_a = [
        Ring("req", r, n, lambda b, m=m: rows_a.at[b, m], ring_sem.at[m]) for m in range(micro)
    ]
    rings_b = [
        Ring("head", h, n, lambda b, m=m: rows_b.at[b, m], ring_sem.at[micro + m])
        for m in range(micro)
    ]
    rings_h = [
        Ring("head", h, n, lambda b, m=m: hidden.at[b, m], ring_sem.at[2 * micro + m])
        for m in range(micro)
    ]

    def settle_a(m):
        first_swaps[m][0].wait_recv()
        settle(first_a.at[m], rows_a.at[r, m])

    def settle_b(m):
        first_swaps[m][1].wait_recv()
        settle(first_b.at[m], rows_b.at[h, m])

    with jax.named_scope("settle"):
        settle_a(0)
        rings_a[0].start()
        settle_b(0)
        rings_b[0].start()
        settle_a(1)
        rings_a[1].start()
        settle_b(1)
        rings_b[1].start()

    def mix():
        logits = jnp.zeros((tokens, 2 * n), F32)
        for j in range(n):
            full = stream_all[j].astype(F32) * aux_all[j].astype(F32)[n : n + 1] * inverse
            for piece in pieces(full):
                logits += dot_t(piece, aux_all[j])
        lane = iota((tokens, 2 * n), 1)
        powers = [
            jnp.exp(jnp.sum(jnp.where(lane == ids[k], logits, F32(0.0)), axis=-1, keepdims=True))
            for k in range(2)
        ]
        total = powers[0] + powers[1]
        return powers[0] / total * chosen_at[0] + powers[1] / total * chosen_at[1]

    def activate(m):
        x = rows_a[:, m].reshape(all_rows, half)
        y = dot(x, wide[pl.ds(0, half), :])
        x = dot(crossed[...], rows_b[:, m].reshape(all_rows, half)).astype(BF16)
        y += dot(x, wide[pl.ds(half, half), :])
        gated, upward = y[:, :hidden_width], y[:, hidden_width:]
        hidden[h, m] = (gated / (1.0 + jnp.exp(-gated)) * upward).astype(BF16)
        rings_h[m].start()

    def lower(b, m, first=False):
        y = dot(
            hidden[b, m], down[pl.ds(pl.multiple_of(b * hidden_width, hidden_width), hidden_width), :]
        ).reshape(n, block_rows, width)
        acc[m] = y if first else acc[m] + y

    def gather_step(m, k):
        rings_a[m].step(k)
        rings_b[m].step(k)

    def hidden_step(m, k, first=False):
        rings_h[m].step(k)
        if first:
            lower(h, m, True)
        for b in rings_h[m].blocks(k):
            lower(b, m)

    swaps_down = [
        Swap(
            "req",
            r,
            n,
            lambda to, m=m: down_send.at[m, to],
            down_recv.at[m],
            swap_sem.at[8 + m],
        )
        for m in range(micro)
    ]

    def hand_over(m):
        down_send[m] = acc[m].astype(BF16)
        swaps_down[m].start()

    def collect(m):
        total = acc[m, r]
        swaps_down[m].wait_recv()
        for d in range(1, n):
            total += down_recv[m, lax.rem(r + d, n)].astype(F32)
        return total.astype(BF16)

    with jax.named_scope("rows"):
        gather_step(0, 1)
        for load in loads[3:]:
            load.wait()
        gather_step(1, 1)
        gather_step(0, 2)
        gather_step(1, 2)
        gather_step(0, 3)
        gather_step(1, 3)
        gather_step(0, 4)
        activate(0)
        gather_step(1, 4)
    with jax.named_scope("hidden_units"):
        activate(1)
        hidden_step(0, 1, True)
        hidden_step(1, 1, True)
        hidden_step(0, 2)
        hidden_step(1, 2)
        hidden_step(0, 3)
        hidden_step(1, 3)
        hidden_step(0, 4)
        hand_over(0)
        hidden_step(1, 4)
        hand_over(1)
        mixing = mix()
        for swap in (swap_att, swap_aux, swap_part, swap_stream, *first_swaps[0], *first_swaps[1]):
            swap.wait_send()
        for ring in rings_a + rings_b + rings_h:
            ring.wait_send()

    with jax.named_scope("collect"):
        expert_rows = jnp.concatenate([collect(m) for m in range(micro)], axis=0)
        back_send[...] = dot(sorted_rows[...], expert_rows).reshape(n, slots, width)

    def back(to, at):
        return pltpu.make_async_remote_copy(
            src_ref=back_send.at[to],
            dst_ref=back_recv.at[at],
            send_sem=back_sem.at[0],
            recv_sem=back_sem.at[1],
            device_id={"head": jnp.int32(to), "exp": h},
            device_id_type=MESH,
        )

    with jax.named_scope("return"):
        for j in range(n):

            @pl.when(jnp.logical_or(h != e, h != j))
            def _():
                back(j, e).start()

            @pl.when(jnp.logical_and(h == e, h == j))
            def _():
                back_recv[j] = back_send[j]

        for swap in swaps_down:
            swap.wait_send()
        for count, here in ((n, h != e), (n - 1, h == e)):

            @pl.when(here)
            def _():
                those = back_recv.at[pl.ds(0, count)]
                every = pltpu.make_async_remote_copy(
                    src_ref=those,
                    dst_ref=those,
                    send_sem=back_sem.at[0],
                    recv_sem=back_sem.at[1],
                    device_id={"exp": lax.rem(e + 1, n)},
                    device_id_type=MESH,
                )
                every.wait_recv()
                every.wait_send()

    returned = back_recv[...].reshape(places, width)
    returned = returned.astype(BF16)
    result = stream_all[e].astype(F32)
    for piece in pieces(mixing):
        result += dot(piece, returned)
    out_ref[...] = result.reshape(micro, group, width).astype(BF16)


def per_device(
    n,
    query,
    cache_keys,
    cache_values,
    lengths,
    out_proj,
    residual,
    norm_gain,
    router,
    expert_ids,
    gate_weight,
    up_weight,
    down_weight,
):
    micro, group, width = query.shape
    tokens, slots = micro * group, micro * SLOTS
    features = n * width
    hidden_width = gate_weight.shape[2]
    vmem = pl.BlockSpec(memory_space=pltpu.VMEM)
    smem = pl.BlockSpec(memory_space=pltpu.SMEM)
    anywhere = pl.BlockSpec(memory_space=pl.ANY)

    block_rows = n * SLOTS
    all_rows = n * block_rows
    scratch = [
        pltpu.VMEM(cache_keys.shape, BF16),
        pltpu.VMEM(cache_values.shape, BF16),
        pltpu.VMEM(out_proj.shape, BF16),
        pltpu.VMEM((features, 2 * hidden_width), BF16),
        pltpu.VMEM(down_weight.shape[1:], BF16),
        pltpu.VMEM((n, 2 * n, width), BF16),
        pltpu.VMEM((n, tokens, width), BF16),
        pltpu.VMEM((n, tokens, width), F32),
        pltpu.VMEM((n, tokens, width), BF16),
        pltpu.VMEM((n, tokens, width), BF16),
        pltpu.VMEM((n, tokens, width), BF16),
        pltpu.VMEM((micro, n, n // 2 * SLOTS, width), BF16),
        pltpu.VMEM((micro, n, n // 2 * SLOTS, width), BF16),
        pltpu.VMEM((n, micro, block_rows, features // 2), BF16),
        pltpu.VMEM((n, micro, block_rows, features // 2), BF16),
        pltpu.VMEM((micro, n // 2 * SLOTS, n // 2 * tokens), BF16),
        pltpu.VMEM((n * n // 2 * SLOTS, n * n // 2 * SLOTS), BF16),
        pltpu.VMEM((all_rows, all_rows), BF16),
        pltpu.VMEM((micro * block_rows, micro * block_rows), BF16),
        pltpu.VMEM((n, micro, all_rows, hidden_width), BF16),
        pltpu.VMEM((micro, n, block_rows, width), F32),
        pltpu.VMEM((micro, n, block_rows, width), BF16),
        pltpu.VMEM((micro, n, block_rows, width), BF16),
        pltpu.VMEM((n, slots, width), F32),
        pltpu.VMEM((n, slots, width), F32),
        pltpu.SemaphoreType.DMA((6,)),
        pltpu.SemaphoreType.DMA((10, 2)),
        pltpu.SemaphoreType.DMA((3 * micro, 4, n // 2)),
        pltpu.SemaphoreType.DMA((2,)),
    ]
    return pl.pallas_call(
        functools.partial(layer, n),
        out_shape=jax.ShapeDtypeStruct((micro, group, width), BF16),
        in_specs=[
            vmem,
            anywhere,
            anywhere,
            smem,
            anywhere,
            vmem,
            vmem,
            vmem,
            vmem,
            anywhere,
            anywhere,
            anywhere,
        ],
        out_specs=vmem,
        scratch_shapes=scratch,
        compiler_params=pltpu.CompilerParams(
            collective_id=0, has_side_effects=True, vmem_limit_bytes=60 * 1024 * 1024
        ),
    )(
        query,
        cache_keys,
        cache_values,
        lengths,
        out_proj,
        residual,
        norm_gain,
        router.T,
        expert_ids.transpose(0, 2, 1),
        gate_weight,
        up_weight,
        down_weight,
    )


def solution(mesh):
    in_specs = (
        P(None, ("req", "exp"), "head"),
        P(None, ("req", "exp"), None, "head"),
        P(None, ("req", "exp"), None, "head"),
        P(None, ("req", "exp")),
        P("head", "exp"),
        P(None, ("req", "head"), "exp"),
        P("exp"),
        P("exp", None),
        P(None, ("req", "head"), None),
        P("exp", None, ("req", "head")),
        P("exp", None, ("req", "head")),
        P("exp", "req", "head"),
    )
    out_specs = P(None, ("req", "head"), "exp")
    return jax.shard_map(
        functools.partial(per_device, mesh.shape["exp"]),
        mesh=mesh,
        in_specs=in_specs,
        out_specs=out_specs,
        check_vma=False,
    )
```
